768 devices in a mesh: row: 48 (over x, z_lo, core), col: 16 (over y, z_hi).
Axes of the slice: x: 4, y: 8, z: 12 (z_hi: 2, z_lo: 6; z = z_hi * 6 + z_lo), core: 2. Of those that a mesh axis runs over, the one named last changes fastest.
Arguments:
- samples: bfloat16 [384, 36864], P('col', 'row'), may hold values from -6 to 6
- cotangent: bfloat16 [384, 24576], P('row', 'col'), may hold values from -12 to 12
- weight: bfloat16 [36864, 24576], P('row', 'col'), may hold values from -0.03125 to 0.03125
- row_second: float32 [36864], P('row'), may hold values from 0.5 to 30
- col_second: float32 [24576], P('col'), may hold values from 1 to 10
Outputs:
- input_grad: bfloat16 [384, 36864], P('col', 'row')
- new_weight: bfloat16 [36864, 24576], P('row', 'col')
- new_row: float32 [36864], P('row')
- new_col: float32 [24576], P('col')
The draws below stay inside these ranges and needn't reach their ends.
All inputs are finite; a program needn't handle non-finite values.
Results may differ from the reference program's by a relative error of at most 0.0029.
The reference program's roundings to bfloat16 on the way (of `slope`) count: a program that leaves them out, or rounds other values in their place, can miss the bound.
Values may be sent and summed in bfloat16 or wider, within the bound.
No kernel may reach another device: no remote copies, remote signals or barrier semaphores. Data moves between devices by JAX's collectives and lax.ppermute only.
A program may use at most 32 MiB of HBM per device.

```python
import math
import jax
import jax.numpy as jnp
from jax import lax

WIN = 36864
WOUT = 24576
B = 384
ADAM_STEP = 10


def draw_row_second(key, part):
    key = jax.random.fold_in(key, 1)
    position = jnp.arange(WIN, dtype=jnp.float32) / WIN
    rough = jnp.exp(jax.random.uniform(key, (WIN,), jnp.float32, 0.0, math.log(3.0)))
    base = jnp.exp(position * math.log(10.0))
    return (base * rough).astype(jnp.float32)


def strengthened(result, key, source, target, blocks, factor):
    def block_of(dim):
        return (jnp.arange(result.shape[dim]) // (result.shape[dim] // blocks)).reshape((-1,) + (1,) * (result.ndim - 1 - dim))

    one_side = jax.random.permutation(key, blocks)[block_of(target)]
    second = (block_of(target) + blocks // 2) % blocks
    return jnp.where((block_of(source) == one_side) | (block_of(source) == second), factor * result, result)


def shard_levels(own_key, extent, split, low, high):
    def one(dim, blocks):
        heights = jax.random.uniform(jax.random.fold_in(jax.random.fold_in(own_key, 6), dim), (blocks,), jnp.float32, low / len(split), high / len(split))
        return jnp.repeat(jnp.exp(heights), extent[dim] // blocks).reshape((-1,) + (1,) * (len(extent) - dim - 1))

    factor_of = one(*split[0])
    for cut in split[1:]:
        factor_of = factor_of * one(*cut)
    return factor_of


def gaussian(rng, shape, deviation, reach, split=(), held_as=jnp.bfloat16):
    values = jax.random.normal(rng, shape, jnp.float32) * deviation
    if len(split) > 0:
        values = shard_levels(rng, shape, split, -0.22, 0.18) * values
    return jnp.clip(values, min=-reach, max=reach).astype(held_as)


def gaussian_with(rng, dims, deviation, bound, pieces, heavy, kind=jnp.bfloat16):
    drawn = deviation * jax.random.normal(rng, dims, jnp.float32)
    if pieces:
        drawn = drawn * shard_levels(rng, dims, pieces, -0.22, 0.18)
    return jnp.clip(strengthened(drawn, jax.random.fold_in(rng, 3), *heavy), -bound, bound).astype(kind)


def setup_inputs(seed: int = 0) -> dict:
    streams_of = jax.random.split(jax.random.key(seed), 6)
    return {
        "samples": gaussian_with(streams_of[0], (B, WIN), 1.0, 6.0, ((0, 16), (1, 48)), (1, 0, 48, 3.25)),
        "cotangent": gaussian_with(streams_of[1], (B, WOUT), 2.0, 12.0, ((0, 48), (1, 16)), (1, 0, 48, 3.25)),
        "weight": gaussian(streams_of[2], (WIN, WOUT), WIN ** -0.5, 0.03125, ((0, 48), (1, 16))),
        "row_second": draw_row_second(jax.random.fold_in(streams_of[5], 71), 0),
        "col_second": jnp.clip(jnp.exp(math.log(10.0) - 2.3025851 * jax.random.uniform(streams_of[4], (WOUT,), jnp.float32) ** shard_levels(streams_of[4], (WOUT,), ((0, 16),), -0.2, 0.2)), 1.0, 10.0),
    }


def silu_slope(preact):
    sig = jax.nn.sigmoid(preact)
    return sig * (1.0 + preact * (1.0 - sig))

def reference(samples, cotangent, weight, row_second, col_second):
    preact = jnp.dot(samples, weight, preferred_element_type=jnp.float32)
    slope = (cotangent.astype(jnp.float32) * silu_slope(preact)).astype(jnp.bfloat16)
    input_grad = jnp.dot(slope, weight.T, preferred_element_type=jnp.float32).astype(jnp.bfloat16)
    grad = jnp.dot(samples.T, slope, preferred_element_type=jnp.float32)
    squared = grad * grad
    new_row = 0.999 * row_second + 0.001 * lax.optimization_barrier(jnp.mean(squared, axis=1))
    new_col = 0.999 * col_second + 0.001 * lax.optimization_barrier(jnp.mean(squared, axis=0))
    scale = jnp.mean(new_row)
    fix_two = 1.0 - 0.999 ** ADAM_STEP
    second = new_row[:, None] * new_col[None, :] / scale
    update = grad / (jnp.sqrt(second / fix_two) + 1e-08)
    new_weight = (weight.astype(jnp.float32) - 0.01 * update).astype(jnp.bfloat16)
    return (input_grad, new_weight, new_row, new_col)
```

```python
import jax
import jax.numpy as jnp
from jax import lax
from jax.sharding import Mesh
from jax.sharding import PartitionSpec as P

WIN = 36864
WOUT = 24576
ADAM_STEP = 10
WEIGHT_MAX = 0.03125
GRAM_SCALE = 1.0 / 32.0

X, ZL, CORE, Y, ZH = 4, 6, 2, 8, 2
ROWS = X * ZL * CORE
COLS = Y * ZH
f32, f16, bf16 = jnp.float32, jnp.float16, jnp.bfloat16


def silu_slope(preact):
    sig = jax.nn.sigmoid(preact)
    return sig * (1.0 + preact * (1.0 - sig))


def exchange(blocks, axis):
    return lax.all_to_all(blocks, axis, 0, 0)


def gather(block, axis, size):
    return exchange(jnp.broadcast_to(block[None], (size,) + block.shape), axis)


def exponent(bound):
    return jnp.ceil(jnp.log2(jnp.maximum(bound, 1e-30))) - 15.0


def split(value, kind):
    info = jnp.finfo(kind)
    high = lax.reduce_precision(value, info.nexp, info.nmant)
    return high.astype(kind), value - high


def split16(value):
    high, rest = split(value, f16)
    return high, (rest * 2048.0).astype(f16)


def local(samples, cotangent, weight, row_second, col_second):
    own, win = samples.shape
    share, wout = cotangent.shape
    batch = own * COLS

    gathered = gather(samples, ("y", "zh"), COLS).reshape(X, ZL, CORE, share, win)
    gathered = gathered.transpose(2, 0, 1, 3, 4).reshape(batch, win)

    partial = jnp.dot(gathered, weight, preferred_element_type=f32)
    gram = lax.dot_general(gathered, gathered, (((1,), (1,)), ((), ())), preferred_element_type=f32)
    sums = jnp.concatenate([partial, gram * GRAM_SCALE], axis=1)
    for axis, size in (("core", CORE), ("x", X), ("zl", ZL)):
        blocks = sums.astype(f16).reshape(size, sums.shape[0] // size, sums.shape[1])
        sums = jnp.sum(exchange(blocks, axis).astype(f32), axis=0)
    slope = (cotangent.astype(f32) * silu_slope(sums[:, :wout])).astype(bf16)

    gram_high, gram_low = split(sums[:, wout:], bf16)
    second_one, rest = split(jnp.sum(row_second), bf16)
    second_two, second_three = split(rest, bf16)
    lanes = lax.broadcasted_iota(jnp.int32, (share, 128), 1)
    seconds = jnp.where(lanes == 0, second_one, jnp.where(lanes == 1, second_two, second_three.astype(bf16)))
    packed = jnp.concatenate([slope, gram_high, gram_low.astype(bf16), seconds], axis=1)
    for axis, size in (("zl", ZL), ("x", X), ("core", CORE)):
        packed = gather(packed, axis, size).reshape(packed.shape[0] * size, packed.shape[1])
    slope = packed[:, :wout]
    gram_high = packed[:, wout : wout + batch]
    gram_low = packed[:, wout + batch : wout + 2 * batch]
    seconds = packed.reshape(ROWS, share, -1)[:, 0, wout + 2 * batch :].astype(f32)
    second_total = jnp.sum(seconds[:, :3])

    mixed = jnp.dot(gram_high, slope, preferred_element_type=f32) + jnp.dot(gram_low, slope, preferred_element_type=f32)
    col_total = jnp.sum(slope.astype(f32) * mixed, axis=0) / GRAM_SCALE
    new_col = 0.999 * col_second + 0.001 * (col_total / WIN)
    all_total = jnp.sum(col_total)

    grad = lax.dot_general(gathered, slope, (((0,), (0,)), ((), ())), preferred_element_type=f32)
    row_total = jnp.sum(grad * grad, axis=1)

    partial = lax.dot_general(slope, weight, (((1,), (1,)), ((), ())), preferred_element_type=f32)
    partial = partial.reshape(CORE, X, ZL, share, win).transpose(1, 2, 0, 3, 4).reshape(COLS, own, win)
    grad_exp = exponent(jnp.max(jnp.abs(slope)).astype(f32) * (WEIGHT_MAX * wout))
    row_exp = exponent(jnp.max(row_total))
    total_exp = exponent(all_total)
    row_high, row_low = split16(row_total * jnp.exp2(-row_exp))
    total_high, total_low = split16(all_total * jnp.exp2(-total_exp))
    scalars = jnp.zeros((128,), f16)
    for i, value in enumerate((grad_exp, row_exp, total_exp, total_high, total_low)):
        scalars = jnp.where(lax.broadcasted_iota(jnp.int32, (128,), 0) == i, value.astype(f16), scalars)
    groups = win // 128
    side = jnp.concatenate(
        [row_high.reshape(groups, 128), row_low.reshape(groups, 128), scalars[None],
         jnp.zeros((own - 2 * groups - 1, 128), f16)], axis=0
    )
    message = jnp.concatenate(
        [(partial * jnp.exp2(-grad_exp)).astype(f16), jnp.broadcast_to(side[None], (COLS, own, 128))], axis=2
    )
    message = exchange(message, ("y", "zh")).astype(f32)
    scalars = message[:, 2 * groups, win:]
    input_grad = jnp.sum(message[:, :, :win] * jnp.exp2(scalars[:, 0])[:, None, None], axis=0).astype(bf16)
    row_parts = message[:, :groups, win:] + message[:, groups : 2 * groups, win:] * (1.0 / 2048.0)
    row_total = jnp.sum(row_parts * jnp.exp2(scalars[:, 1])[:, None, None], axis=0).reshape(win)
    all_total = jnp.sum((scalars[:, 3] + scalars[:, 4] * (1.0 / 2048.0)) * jnp.exp2(scalars[:, 2]))

    new_row = 0.999 * row_second + 0.001 * (row_total / WOUT)
    scale = 0.999 * (second_total / WIN) + 0.001 * (all_total / WOUT / WIN)
    fix_two = 1.0 - 0.999**ADAM_STEP
    row_root = jnp.sqrt(new_row / (scale * fix_two))
    col_root = jnp.sqrt(new_col)
    update = grad / (row_root[:, None] * col_root[None, :] + 1e-08)
    new_weight = (weight.astype(f32) - 0.01 * update).astype(bf16)
    return (input_grad, new_weight, new_row, new_col)


def solution(mesh):
    fine = Mesh(mesh.devices.reshape(X, ZL, CORE, Y, ZH), ("x", "zl", "core", "y", "zh"))
    row, col = ("x", "zl", "core"), ("y", "zh")
    in_specs = (P(col, row), P(row, col), P(row, col), P(row), P(col))
    out_specs = (P(col, row), P(row, col), P(row), P(col))
    return jax.shard_map(local, mesh=fine, in_specs=in_specs, out_specs=out_specs, check_vma=False)
```

```python
import jax
import jax.numpy as jnp
from jax import lax
from jax.experimental import pallas as pl
from jax.experimental.pallas import tpu as pltpu
from jax.sharding import Mesh
from jax.sharding import PartitionSpec as P

WIN = 36864
WOUT = 24576
ADAM_STEP = 10
WEIGHT_MAX = 0.03125
GRAM_SCALE = 1.0 / 32.0

X, ZL, CORE, Y, ZH = 4, 6, 2, 8, 2
ROWS = X * ZL * CORE
COLS = Y * ZH
f32, f16, bf16 = jnp.float32, jnp.float16, jnp.bfloat16


def silu_slope(preact):
    sig = jax.nn.sigmoid(preact)
    return sig * (1.0 + preact * (1.0 - sig))


def exchange(blocks, axis):
    return lax.all_to_all(blocks, axis, 0, 0)


def gather(block, axis, size):
    return exchange(jnp.broadcast_to(block[None], (size,) + block.shape), axis)


def exponent(bound):
    return jnp.ceil(jnp.log2(jnp.maximum(bound, 1e-30))) - 15.0


def split(value):
    high = lax.reduce_precision(value, 8, 7)
    return high.astype(bf16), value - high


def whole(value):
    return jnp.sum(jnp.sum(value, axis=0, keepdims=True), axis=1, keepdims=True)


NT = (((1,), (1,)), ((), ()))


def message_kernel(packed_ref, samples_ref, weight_ref, message_ref, partial_ref):
    batch, win = samples_ref.shape
    wout = weight_ref.shape[1]
    own = batch // COLS
    share = batch // ROWS
    slope = packed_ref[:, :wout]
    gram = packed_ref[:, wout : wout + batch].astype(f32) + packed_ref[:, wout + batch : wout + 2 * batch].astype(f32)
    partial_ref[...] = lax.dot_general(slope, weight_ref[...], NT, preferred_element_type=f32)
    mixed = lax.dot_general(slope, slope, NT, preferred_element_type=f32)
    total = whole(mixed * gram) * (1.0 / GRAM_SCALE)
    mixed_high = mixed.astype(bf16)
    mixed_low = (mixed - mixed_high.astype(f32)).astype(bf16)
    samples = samples_ref[...]
    spread = jnp.dot(mixed_high, samples, preferred_element_type=f32)
    spread += jnp.dot(mixed_low, samples, preferred_element_type=f32)
    row_total = jnp.sum(samples.astype(f32) * spread, axis=0, keepdims=True)

    top = jnp.max(jnp.max(jnp.abs(slope), axis=0, keepdims=True).astype(f32), axis=1, keepdims=True)
    grad_exp = exponent(top * (WEIGHT_MAX * wout))
    row_exp = exponent(jnp.max(row_total, axis=1, keepdims=True))
    total_exp = exponent(total)
    rows = row_total * jnp.exp2(-row_exp)
    rows = jnp.concatenate([rows[:, 128 * i : 128 * (i + 1)] for i in range(win // 128)], axis=0)
    rows_high = rows.astype(bf16).astype(f32)
    total = total * jnp.exp2(-total_exp)
    total_high = total.astype(bf16).astype(f32)
    lanes = lax.broadcasted_iota(jnp.int32, (1, 128), 1)
    scalars = jnp.zeros((1, 128), f32)
    for i, value in enumerate((grad_exp, row_exp, total_exp, total_high, (total - total_high) * 256.0)):
        scalars = jnp.where(lanes == i, value, scalars)
    pad = jnp.zeros((own - 2 * (win // 128) - 1, 128), f32)
    side = jnp.concatenate([rows_high, (rows - rows_high) * 256.0, scalars, pad], axis=0)
    factor = jnp.exp2(-grad_exp)
    each = own // share
    for dest in range(COLS):
        blocks = []
        for block in range(dest * each, (dest + 1) * each):
            first = ((block % CORE) * (ROWS // CORE) + block // CORE) * share
            blocks.append(partial_ref[first : first + share, :])
        message_ref[dest, :, :win] = jnp.concatenate(blocks, axis=0) * factor
        message_ref[dest, :, win:] = side


def make_message(packed, samples, weight):
    batch, win = samples.shape
    return pl.pallas_call(
        message_kernel,
        out_shape=jax.ShapeDtypeStruct((COLS, batch // COLS, win + 128), f32),
        in_specs=[pl.BlockSpec(memory_space=pltpu.VMEM)] * 3,
        out_specs=pl.BlockSpec(memory_space=pltpu.VMEM),
        scratch_shapes=[pltpu.VMEM((batch, win), f32)],
        compiler_params=pltpu.CompilerParams(vmem_limit_bytes=40 << 20),
    )(packed, samples, weight)


def update_kernel(message_ref, packed_ref, transposed_ref, weight_ref, row_second_ref, seconds_ref, col_root_ref,
                  input_grad_ref, new_row_ref, new_weight_ref, root_ref):
    win = row_second_ref.shape[1]
    wout = weight_ref.shape[1]
    groups = win // 128
    rows = weight_ref.shape[0]
    step = pl.program_id(0)

    @pl.when(step == 0)
    def _():
        total = jnp.zeros((1, 1), f32)
        sums = jnp.zeros((groups, 128), f32)
        grads = jnp.zeros(input_grad_ref.shape, f32)
        for source in range(COLS):
            side = message_ref[source, :, win:]
            scalars = side[2 * groups : 2 * groups + 1, :]
            powers = jnp.exp2(scalars[:, :3])
            grads += message_ref[source, :, :win] * powers[:, 0:1]
            sums += (side[:groups] + side[groups : 2 * groups] * (1.0 / 256.0)) * powers[:, 1:2]
            total += (scalars[:, 3:4] + scalars[:, 4:5] * (1.0 / 256.0)) * powers[:, 2:3]
        input_grad_ref[...] = grads.astype(bf16)
        row_total = jnp.concatenate([sums[i : i + 1] for i in range(groups)], axis=1)
        new_row = 0.999 * row_second_ref[...] + 0.001 * (row_total / WOUT)
        new_row_ref[...] = new_row
        scale = 0.999 * (seconds_ref[...] / WIN) + 0.001 * (total / WOUT / WIN)
        root = jnp.sqrt(new_row / (scale * (1.0 - 0.999**ADAM_STEP)))
        root_ref[...] = jnp.transpose(jnp.broadcast_to(root, (128, win)))

    grad = jnp.dot(transposed_ref[...], packed_ref[:, :wout], preferred_element_type=f32)
    root = root_ref[pl.ds(pl.multiple_of(step * rows, rows), rows), :]
    for i in range(0, wout, 128):
        bottom = root * col_root_ref[:, i : i + 128] + 1e-08
        change = 0.01 * grad[:, i : i + 128] / bottom
        new_weight_ref[:, i : i + 128] = (weight_ref[:, i : i + 128].astype(f32) - change).astype(bf16)


def update(message, packed, transposed, weight, row_second, seconds, col_root):
    win, wout = weight.shape
    rows = 256
    whole_in = [pl.BlockSpec(memory_space=pltpu.VMEM)]
    return pl.pallas_call(
        update_kernel,
        grid=(win // rows,),
        out_shape=(
            jax.ShapeDtypeStruct((message.shape[1], win), bf16),
            jax.ShapeDtypeStruct((1, win), f32),
            jax.ShapeDtypeStruct((win, wout), bf16),
        ),
        in_specs=whole_in * 2
        + [pl.BlockSpec((rows, transposed.shape[1]), lambda i: (i, 0)), pl.BlockSpec((rows, wout), lambda i: (i, 0))]
        + whole_in * 3,
        out_specs=(
            pl.BlockSpec((message.shape[1], win), lambda i: (0, 0)),
            pl.BlockSpec((1, win), lambda i: (0, 0)),
            pl.BlockSpec((rows, wout), lambda i: (i, 0)),
        ),
        scratch_shapes=[pltpu.VMEM((win, 128), f32)],
        compiler_params=pltpu.CompilerParams(vmem_limit_bytes=40 << 20),
    )(message, packed, transposed, weight, row_second[None], seconds, col_root)


def local(samples, cotangent, weight, row_second, col_second):
    own, win = samples.shape
    share, wout = cotangent.shape
    batch = own * COLS

    gathered = gather(samples, ("y", "zh"), COLS).reshape(X, ZL, CORE, share, win)
    gathered = gathered.transpose(2, 0, 1, 3, 4).reshape(batch, win)

    partial = jnp.dot(gathered, weight, preferred_element_type=f32)
    gram = lax.dot_general(gathered, gathered, (((1,), (1,)), ((), ())), preferred_element_type=f32)
    sums = jnp.concatenate([partial, gram * GRAM_SCALE], axis=1)
    for axis, size in (("core", CORE), ("x", X), ("zl", ZL)):
        blocks = sums.astype(f16).reshape(size, sums.shape[0] // size, sums.shape[1])
        sums = jnp.sum(exchange(blocks, axis).astype(f32), axis=0)
    slope = (cotangent.astype(f32) * silu_slope(sums[:, :wout])).astype(bf16)

    gram_high, gram_low = split(sums[:, wout:])
    second_one, rest = split(jnp.sum(row_second))
    second_two, second_three = split(rest)
    lanes = lax.broadcasted_iota(jnp.int32, (share, 128), 1)
    seconds = jnp.where(lanes == 0, second_one, jnp.where(lanes == 1, second_two, second_three.astype(bf16)))
    packed = jnp.concatenate([slope, gram_high, gram_low.astype(bf16), seconds], axis=1)
    for axis, size in (("zl", ZL), ("x", X), ("core", CORE)):
        packed = gather(packed, axis, size).reshape(packed.shape[0] * size, packed.shape[1])

    message = exchange(make_message(packed, gathered, weight).astype(f16), ("y", "zh")).astype(f32)

    slope = packed[:, :wout]
    mixed = jnp.dot(packed[:, wout : wout + batch], slope, preferred_element_type=f32)
    mixed += jnp.dot(packed[:, wout + batch : wout + 2 * batch], slope, preferred_element_type=f32)
    col_total = jnp.sum(slope.astype(f32) * mixed, axis=0) / GRAM_SCALE
    new_col = 0.999 * col_second + 0.001 * (col_total / WIN)
    seconds = packed.reshape(ROWS, share, -1)[:, 0, wout + 2 * batch :].astype(f32)
    seconds = jnp.sum(seconds[:, :3]).reshape(1, 1)
    input_grad, new_row, new_weight = update(
        message, packed, gathered.T, weight, row_second, seconds, jnp.sqrt(new_col)[None]
    )
    return (input_grad, new_weight, new_row[0], new_col)


def solution(mesh):
    fine = Mesh(mesh.devices.reshape(X, ZL, CORE, Y, ZH), ("x", "zl", "core", "y", "zh"))
    row, col = ("x", "zl", "core"), ("y", "zh")
    in_specs = (P(col, row), P(row, col), P(row, col), P(row), P(col))
    out_specs = (P(col, row), P(row, col), P(row), P(col))
    return jax.shard_map(local, mesh=fine, in_specs=in_specs, out_specs=out_specs, check_vma=False)
```

```python
import jax
import jax.numpy as jnp
from jax import lax
from jax.experimental import pallas as pl
from jax.experimental.pallas import tpu as pltpu
from jax.sharding import Mesh
from jax.sharding import PartitionSpec as P

WIN = 36864
WOUT = 24576
ADAM_STEP = 10
WEIGHT_MAX = 0.03125
GRAM_SCALE = 1.0 / 32.0

X, ZL, CORE, Y, ZH = 4, 6, 2, 8, 2
ROWS = X * ZL * CORE
COLS = Y * ZH
f32, f16, bf16 = jnp.float32, jnp.float16, jnp.bfloat16


def silu_slope(preact):
    sig = jax.nn.sigmoid(preact)
    return sig * (1.0 + preact * (1.0 - sig))


def exchange(blocks, axis):
    return lax.all_to_all(blocks, axis, 0, 0)


def gather(block, axis, size):
    return exchange(jnp.broadcast_to(block[None], (size,) + block.shape), axis)


def exponent(bound):
    return jnp.ceil(jnp.log2(jnp.maximum(bound, 1e-30))) - 15.0


def split(value):
    high = lax.reduce_precision(value, 8, 7)
    return high.astype(bf16), value - high


def whole(value):
    return jnp.sum(jnp.sum(value, axis=0, keepdims=True), axis=1, keepdims=True)


NT = (((1,), (1,)), ((), ()))


def halves(batch):
    return batch // 2 + batch // ROWS


def pack_kernel(place_ref, sums_ref, cotangent_ref, row_second_ref, packed_ref):
    share, wout = cotangent_ref.shape
    batch = sums_ref.shape[1] - wout
    side = packed_ref.shape[1] - wout
    count = halves(batch)
    packed_ref[:, :wout] = (cotangent_ref[...].astype(f32) * silu_slope(sums_ref[:, :wout])).astype(bf16)
    shift = lax.rem(batch - place_ref[0] * share, batch)
    gram = pltpu.roll(sums_ref[:, wout:], shift, 1)
    gram = jnp.concatenate([gram, jnp.zeros((share, side - batch), f32)], axis=1)
    high = gram.astype(bf16).astype(f32)
    low = pltpu.roll(gram - high, count, 1)
    lanes = lax.broadcasted_iota(jnp.int32, (share, side), 1)
    out = jnp.where(lanes < count, high, jnp.where(lanes < 2 * count, low, 0.0))
    rest = whole(row_second_ref[...])
    for i in range(3):
        part = rest.astype(bf16).astype(f32)
        rest = rest - part
        out = jnp.where(lanes == 2 * count + i, part, out)
    packed_ref[:, wout:] = out.astype(bf16)


def pack(place, sums, cotangent, row_second):
    share, wout = cotangent.shape
    width = wout + -(-(2 * halves(sums.shape[1] - wout) + 3) // 128) * 128
    return pl.pallas_call(
        pack_kernel,
        out_shape=jax.ShapeDtypeStruct((share, width), bf16),
        in_specs=[pl.BlockSpec(memory_space=pltpu.SMEM)] + [pl.BlockSpec(memory_space=pltpu.VMEM)] * 3,
        out_specs=pl.BlockSpec(memory_space=pltpu.VMEM),
        compiler_params=pltpu.CompilerParams(vmem_limit_bytes=16 << 20),
    )(place, sums, cotangent, row_second)


def message_kernel(packed_ref, samples_ref, weight_ref, message_ref, gram_ref, partial_ref):
    batch, win = samples_ref.shape
    wout = weight_ref.shape[1]
    own = batch // COLS
    share = batch // ROWS
    slope = packed_ref[:, :wout]
    count = halves(batch)
    lanes = lax.broadcasted_iota(jnp.int32, (share, batch), 1)
    times = jnp.where(lanes < share, 1.0, jnp.where(lanes < batch // 2, 2.0, jnp.where(lanes < count, 1.0, 0.0)))
    packed_half = packed_ref[:, wout:].astype(f32)
    for place in range(ROWS):
        half = packed_half[place * share : (place + 1) * share, :]
        half = half + pltpu.roll(half, half.shape[1] - count, 1)
        gram_ref[place * share : (place + 1) * share, :] = pltpu.roll(half[:, :batch] * times, place * share, 1)
    gram = gram_ref[...]
    partial_ref[...] = lax.dot_general(slope, weight_ref[...], NT, preferred_element_type=f32)
    mixed = lax.dot_general(slope, slope, NT, preferred_element_type=f32)
    total = whole(mixed * gram) * (1.0 / GRAM_SCALE)
    mixed_high = mixed.astype(bf16)
    mixed_low = (mixed - mixed_high.astype(f32)).astype(bf16)
    samples = samples_ref[...]
    spread = jnp.dot(mixed_high, samples, preferred_element_type=f32)
    spread += jnp.dot(mixed_low, samples, preferred_element_type=f32)
    row_total = jnp.sum(samples.astype(f32) * spread, axis=0, keepdims=True)

    top = jnp.max(jnp.max(jnp.abs(slope), axis=0, keepdims=True).astype(f32), axis=1, keepdims=True)
    grad_exp = exponent(top * (WEIGHT_MAX * wout))
    row_exp = exponent(jnp.max(row_total, axis=1, keepdims=True))
    total_exp = exponent(total)
    rows = row_total * jnp.exp2(-row_exp)
    rows = jnp.concatenate([rows[:, 128 * i : 128 * (i + 1)] for i in range(win // 128)], axis=0)
    rows_high = rows.astype(bf16).astype(f32)
    total = total * jnp.exp2(-total_exp)
    total_high = total.astype(bf16).astype(f32)
    lanes = lax.broadcasted_iota(jnp.int32, (1, 128), 1)
    scalars = jnp.zeros((1, 128), f32)
    for i, value in enumerate((grad_exp, row_exp, total_exp, total_high, (total - total_high) * 256.0)):
        scalars = jnp.where(lanes == i, value, scalars)
    pad = jnp.zeros((own - 2 * (win // 128) - 1, 128), f32)
    side = jnp.concatenate([rows_high, (rows - rows_high) * 256.0, scalars, pad], axis=0)
    factor = jnp.exp2(-grad_exp)
    each = own // share
    for dest in range(COLS):
        blocks = []
        for block in range(dest * each, (dest + 1) * each):
            first = ((block % CORE) * (ROWS // CORE) + block // CORE) * share
            blocks.append(partial_ref[first : first + share, :])
        message_ref[dest, :, :win] = jnp.concatenate(blocks, axis=0) * factor
        message_ref[dest, :, win:] = side


def make_message(packed, samples, weight):
    batch, win = samples.shape
    return pl.pallas_call(
        message_kernel,
        out_shape=(
            jax.ShapeDtypeStruct((COLS, batch // COLS, win + 128), f32),
            jax.ShapeDtypeStruct((batch, batch), f32),
        ),
        in_specs=[pl.BlockSpec(memory_space=pltpu.VMEM)] * 3,
        out_specs=(pl.BlockSpec(memory_space=pltpu.VMEM),) * 2,
        scratch_shapes=[pltpu.VMEM((batch, win), f32)],
        compiler_params=pltpu.CompilerParams(vmem_limit_bytes=20 << 20),
    )(packed, samples, weight)


CHUNKS = 3


def update_kernel(message_ref, packed_ref, transposed_ref, weight_ref, row_second_ref, seconds_ref, col_root_ref,
                  input_grad_ref, new_row_ref, new_weight_ref, root_ref, old_ref, new_ref, old_sems, new_sems):
    win, wout = old_ref.shape
    groups = win // 128
    rows = win // CHUNKS

    def fetch(i):
        part = pl.ds(i * rows, rows)
        return pltpu.make_async_copy(weight_ref.at[part], old_ref.at[part], old_sems.at[i])

    def store(i):
        part = pl.ds(i * rows, rows)
        return pltpu.make_async_copy(new_ref.at[part], new_weight_ref.at[part], new_sems.at[i])

    for i in range(CHUNKS):
        fetch(i).start()
    total = jnp.zeros((1, 1), f32)
    sums = jnp.zeros((groups, 128), f32)
    grads = jnp.zeros(input_grad_ref.shape, f32)
    for source in range(COLS):
        side = message_ref[source, :, win:]
        scalars = side[2 * groups : 2 * groups + 1, :]
        powers = jnp.exp2(scalars[:, :3])
        grads += message_ref[source, :, :win] * powers[:, 0:1]
        sums += (side[:groups] + side[groups : 2 * groups] * (1.0 / 256.0)) * powers[:, 1:2]
        total += (scalars[:, 3:4] + scalars[:, 4:5] * (1.0 / 256.0)) * powers[:, 2:3]
    input_grad_ref[...] = grads.astype(bf16)
    new_row = 0.999 * row_second_ref[...] + 0.001 * (sums / WOUT)
    new_row_ref[...] = new_row
    scale = 0.999 * (seconds_ref[...] / WIN) + 0.001 * (total / WOUT / WIN)
    root = jnp.sqrt(new_row / (scale * (1.0 - 0.999**ADAM_STEP)))
    for i in range(groups):
        root_ref[128 * i : 128 * (i + 1), :] = jnp.transpose(jnp.broadcast_to(root[i : i + 1], (128, 128)))

    for i in range(CHUNKS):
        part = slice(i * rows, (i + 1) * rows)
        grad = jnp.dot(transposed_ref[part, :], packed_ref[:, :wout], preferred_element_type=f32)
        root = root_ref[part, :]
        fetch(i).wait()
        for j in range(0, wout, 128):
            bottom = root * col_root_ref[:, j : j + 128] + 1e-08
            change = 0.01 * grad[:, j : j + 128] / bottom
            new_ref[part, j : j + 128] = (old_ref[part, j : j + 128].astype(f32) - change).astype(bf16)
        store(i).start()
    for i in range(CHUNKS):
        store(i).wait()


def update(message, packed, transposed, weight, row_second, seconds, col_root):
    win, wout = weight.shape
    inside, outside = pl.BlockSpec(memory_space=pltpu.VMEM), pl.BlockSpec(memory_space=pltpu.HBM)
    return pl.pallas_call(
        update_kernel,
        out_shape=(
            jax.ShapeDtypeStruct((message.shape[1], win), bf16),
            jax.ShapeDtypeStruct((win // 128, 128), f32),
            jax.ShapeDtypeStruct((win, wout), bf16),
        ),
        in_specs=[inside, inside, inside, outside, inside, inside, inside],
        out_specs=(inside, inside, outside),
        scratch_shapes=[
            pltpu.VMEM((win, 128), f32),
            pltpu.VMEM((win, wout), bf16),
            pltpu.VMEM((win, wout), bf16),
            pltpu.SemaphoreType.DMA((CHUNKS,)),
            pltpu.SemaphoreType.DMA((CHUNKS,)),
        ],
        compiler_params=pltpu.CompilerParams(vmem_limit_bytes=24 << 20),
    )(message, packed, transposed, weight, row_second.reshape(-1, 128), seconds, col_root)


def local(samples, cotangent, weight, row_second, col_second):
    own, win = samples.shape
    share, wout = cotangent.shape
    batch = own * COLS

    gathered = gather(samples, ("y", "zh"), COLS).reshape(X, ZL, CORE, share, win)
    gathered = gathered.transpose(2, 0, 1, 3, 4).reshape(batch, win)

    partial = jnp.dot(gathered, weight, preferred_element_type=f32)
    gram = lax.dot_general(gathered, gathered, (((1,), (1,)), ((), ())), preferred_element_type=f32)
    sums = jnp.concatenate([partial, gram * GRAM_SCALE], axis=1)
    for axis, size in (("core", CORE), ("x", X), ("zl", ZL)):
        blocks = sums.astype(f16).reshape(size, sums.shape[0] // size, sums.shape[1])
        sums = jnp.sum(exchange(blocks, axis).astype(f32), axis=0)

    place = (lax.axis_index("core") * X + lax.axis_index("x")) * ZL + lax.axis_index("zl")
    packed = pack(place.astype(jnp.int32)[None], sums, cotangent, row_second.reshape(-1, 128))
    for axis, size in (("zl", ZL), ("x", X), ("core", CORE)):
        packed = gather(packed, axis, size).reshape(packed.shape[0] * size, packed.shape[1])

    message, gram = make_message(packed, gathered, weight)
    message = exchange(message.astype(f16), ("y", "zh")).astype(f32)

    slope = packed[:, :wout]
    gram_high, gram_low = split(gram)
    mixed = jnp.dot(gram_high, slope, preferred_element_type=f32)
    mixed += jnp.dot(gram_low.astype(bf16), slope, preferred_element_type=f32)
    col_total = jnp.sum(slope.astype(f32) * mixed, axis=0) / GRAM_SCALE
    new_col = 0.999 * col_second + 0.001 * (col_total / WIN)
    seconds = packed.reshape(ROWS, share, -1)[:, 0, wout + 2 * halves(batch) :].astype(f32)
    seconds = jnp.sum(seconds[:, :3]).reshape(1, 1)
    input_grad, new_row, new_weight = update(
        message, packed, gathered.T, weight, row_second, seconds, jnp.sqrt(new_col)[None]
    )
    return (input_grad, new_weight, new_row.reshape(win), new_col)


def solution(mesh):
    fine = Mesh(mesh.devices.reshape(X, ZL, CORE, Y, ZH), ("x", "zl", "core", "y", "zh"))
    row, col = ("x", "zl", "core"), ("y", "zh")
    in_specs = (P(col, row), P(row, col), P(row, col), P(row), P(col))
    out_specs = (P(col, row), P(row, col), P(row), P(col))
    return jax.shard_map(local, mesh=fine, in_specs=in_specs, out_specs=out_specs, check_vma=False)
```

```python
import jax
import jax.numpy as jnp
from jax import lax
from jax.experimental import pallas as pl
from jax.experimental.pallas import tpu as pltpu
from jax.sharding import Mesh
from jax.sharding import PartitionSpec as P

WIN = 36864
WOUT = 24576
ADAM_STEP = 10
WEIGHT_MAX = 0.03125
GRAM_SCALE = 1.0 / 32.0

X, ZL, CORE, Y, ZH = 4, 6, 2, 8, 2
ROWS = X * ZL * CORE
COLS = Y * ZH
f32, f16, bf16 = jnp.float32, jnp.float16, jnp.bfloat16


def silu_slope(preact):
    sig = jax.nn.sigmoid(preact)
    return sig * (1.0 + preact * (1.0 - sig))


def exchange(blocks, axis):
    return lax.all_to_all(blocks, axis, 0, 0)


def gather(block, axis, size):
    return exchange(jnp.broadcast_to(block[None], (size,) + block.shape), axis)


def exponent(bound):
    return jnp.ceil(jnp.log2(jnp.maximum(bound, 1e-30))) - 15.0


def split(value):
    high = lax.reduce_precision(value, 8, 7)
    return high.astype(bf16), value - high


def whole(value):
    return jnp.sum(jnp.sum(value, axis=0, keepdims=True), axis=1, keepdims=True)


def encode(own, grad_exp, rows, total):
    row_exp = exponent(jnp.max(jnp.max(rows, axis=0, keepdims=True), axis=1, keepdims=True))
    total_exp = exponent(total)
    rows = rows * jnp.exp2(-row_exp)
    rows_high = rows.astype(bf16).astype(f32)
    total = total * jnp.exp2(-total_exp)
    total_high = total.astype(bf16).astype(f32)
    lanes = lax.broadcasted_iota(jnp.int32, (1, 128), 1)
    scalars = jnp.zeros((1, 128), f32)
    for i, value in enumerate((grad_exp, row_exp, total_exp, total_high, (total - total_high) * 256.0)):
        scalars = jnp.where(lanes == i, value, scalars)
    pad = jnp.zeros((own - 2 * rows.shape[0] - 1, 128), f32)
    return jnp.concatenate([rows_high, (rows - rows_high) * 256.0, scalars, pad], axis=0)


NT = (((1,), (1,)), ((), ()))


def halves(batch):
    return batch // 2 + batch // ROWS


def pack_kernel(place_ref, sums_ref, cotangent_ref, row_second_ref, packed_ref):
    share, wout = cotangent_ref.shape
    batch = sums_ref.shape[1] - wout
    side = packed_ref.shape[1] - wout
    count = halves(batch)
    packed_ref[:, :wout] = (cotangent_ref[...].astype(f32) * silu_slope(sums_ref[:, :wout])).astype(bf16)
    shift = lax.rem(batch - place_ref[0] * share, batch)
    gram = pltpu.roll(sums_ref[:, wout:], shift, 1)
    gram = jnp.concatenate([gram, jnp.zeros((share, side - batch), f32)], axis=1)
    high = gram.astype(bf16).astype(f32)
    low = pltpu.roll(gram - high, count, 1)
    lanes = lax.broadcasted_iota(jnp.int32, (share, side), 1)
    out = jnp.where(lanes < count, high, jnp.where(lanes < 2 * count, low, 0.0))
    rest = whole(row_second_ref[...])
    for i in range(3):
        part = rest.astype(bf16).astype(f32)
        rest = rest - part
        out = jnp.where(lanes == 2 * count + i, part, out)
    packed_ref[:, wout:] = out.astype(bf16)


def pack(place, sums, cotangent, row_second):
    share, wout = cotangent.shape
    width = wout + -(-(2 * halves(sums.shape[1] - wout) + 3) // 128) * 128
    return pl.pallas_call(
        pack_kernel,
        out_shape=jax.ShapeDtypeStruct((share, width), bf16),
        in_specs=[pl.BlockSpec(memory_space=pltpu.SMEM)] + [pl.BlockSpec(memory_space=pltpu.VMEM)] * 3,
        out_specs=pl.BlockSpec(memory_space=pltpu.VMEM),
        compiler_params=pltpu.CompilerParams(vmem_limit_bytes=16 << 20),
    )(place, sums, cotangent, row_second)


def message_kernel(core_ref, mine_ref, other_ref, samples_ref, weight_ref,
                   message_ref, seconds_ref, slope_ref, gram_ref, partial_ref):
    batch, win = samples_ref.shape
    wout = weight_ref.shape[1]
    own = batch // COLS
    share = batch // ROWS
    half = batch // CORE
    first = core_ref[0] == 0
    packed_half = []
    for i, (low, high) in enumerate(((mine_ref, other_ref), (other_ref, mine_ref))):
        both = jnp.where(first, low[...], high[...])
        slope_ref[i * half : (i + 1) * half, :] = both[:, :wout]
        packed_half.append(both[:, wout:].astype(f32))
    packed_half = jnp.concatenate(packed_half, axis=0)
    slope = slope_ref[...]
    partial_ref[...] = lax.dot_general(slope, weight_ref[...], NT, preferred_element_type=f32)
    count = halves(batch)
    lanes = lax.broadcasted_iota(jnp.int32, packed_half.shape, 1)
    there = (lanes >= 2 * count) & (lanes < 2 * count + 3)
    seconds_ref[...] = whole(jnp.where(there, packed_half, 0.0)) * (1.0 / share)
    lanes = lax.broadcasted_iota(jnp.int32, (share, batch), 1)
    times = jnp.where(lanes < share, 1.0, jnp.where(lanes < batch // 2, 2.0, jnp.where(lanes < count, 1.0, 0.0)))
    for place in range(ROWS):
        piece = packed_half[place * share : (place + 1) * share, :]
        piece = piece + pltpu.roll(piece, piece.shape[1] - count, 1)
        gram_ref[place * share : (place + 1) * share, :] = pltpu.roll(piece[:, :batch] * times, place * share, 1)
    gram = gram_ref[...]
    partial_ref[...] = lax.dot_general(slope, weight_ref[...], NT, preferred_element_type=f32)
    mixed = lax.dot_general(slope, slope, NT, preferred_element_type=f32)
    total = whole(mixed * gram) * (1.0 / GRAM_SCALE)
    mixed_high = mixed.astype(bf16)
    mixed_low = (mixed - mixed_high.astype(f32)).astype(bf16)
    samples = samples_ref[...]
    spread = jnp.dot(mixed_high, samples, preferred_element_type=f32)
    spread += jnp.dot(mixed_low, samples, preferred_element_type=f32)
    row_total = jnp.sum(samples.astype(f32) * spread, axis=0, keepdims=True)

    top = jnp.max(jnp.max(jnp.abs(slope), axis=0, keepdims=True).astype(f32), axis=1, keepdims=True)
    grad_exp = exponent(top * (WEIGHT_MAX * wout))
    rows = jnp.concatenate([row_total[:, 128 * i : 128 * (i + 1)] for i in range(win // 128)], axis=0)
    side = encode(own, grad_exp, rows, total)
    factor = jnp.exp2(-grad_exp)
    each = own // share
    for dest in range(COLS):
        blocks = []
        for block in range(dest * each, (dest + 1) * each):
            start = ((block % CORE) * (ROWS // CORE) + block // CORE) * share
            blocks.append(partial_ref[start : start + share, :])
        message_ref[dest, :, :win] = jnp.concatenate(blocks, axis=0) * factor
        message_ref[dest, :, win:] = side


INSIDE, OUTSIDE = pl.BlockSpec(memory_space=pltpu.VMEM), pl.BlockSpec(memory_space=pltpu.HBM)
SCALAR = pl.BlockSpec(memory_space=pltpu.SMEM)


def make_message(core, mine, other, samples, weight):
    batch, win = samples.shape
    return pl.pallas_call(
        message_kernel,
        out_shape=(
            jax.ShapeDtypeStruct((COLS, batch // COLS, win + 128), f32),
            jax.ShapeDtypeStruct((1, 1), f32),
            jax.ShapeDtypeStruct((batch, weight.shape[1]), bf16),
            jax.ShapeDtypeStruct((batch, batch), f32),
        ),
        in_specs=[SCALAR] + [INSIDE] * 4,
        out_specs=(INSIDE,) * 4,
        scratch_shapes=[pltpu.VMEM((batch, win), f32)],
        compiler_params=pltpu.CompilerParams(vmem_limit_bytes=20 << 20),
    )(core, mine, other, samples, weight)


def decode(pieces):
    own, width = pieces[0].shape
    win = width - 128
    groups = win // 128
    scalars = jnp.concatenate([piece[2 * groups : 2 * groups + 1, win:] for piece in pieces], axis=0)
    powers = jnp.exp2(scalars)
    grads = jnp.zeros((own, win), f32)
    sums = jnp.zeros((groups, 128), f32)
    for i, piece in enumerate(pieces):
        grads += piece[:, :win] * powers[i : i + 1, 0:1]
        side = piece[: 2 * groups, win:]
        sums += (side[:groups] + side[groups:] * (1.0 / 256.0)) * powers[i : i + 1, 1:2]
    total = whole((scalars[:, 3:4] + scalars[:, 4:5] * (1.0 / 256.0)) * powers[:, 2:3])
    return grads, sums, total, jnp.max(scalars[:, 0:1], axis=0, keepdims=True)


def decode_kernel(zh_ref, message_ref, keep_ref, send_ref):
    zh = zh_ref[0]
    grads, sums, total, _ = decode([message_ref[i, zh] for i in range(Y)])
    own, win = grads.shape
    keep_ref[:, :win] = grads
    lanes = lax.broadcasted_iota(jnp.int32, (1, 128), 1)
    rows = [sums, jnp.where(lanes == 0, total, 0.0), jnp.zeros((own - sums.shape[0] - 1, 128), f32)]
    keep_ref[:, win:] = jnp.concatenate(rows, axis=0)
    grads, sums, total, grad_exp = decode([message_ref[i, 1 - zh] for i in range(Y)])
    grad_exp += 3.0
    send_ref[:, :win] = grads * jnp.exp2(-grad_exp)
    send_ref[:, win:] = encode(own, grad_exp, sums, total)


def decoded(zh, message):
    return pl.pallas_call(
        decode_kernel,
        out_shape=(jax.ShapeDtypeStruct(message.shape[2:], f32),) * 2,
        in_specs=[SCALAR, INSIDE],
        out_specs=(INSIDE,) * 2,
        compiler_params=pltpu.CompilerParams(vmem_limit_bytes=12 << 20),
    )(zh, message)


CHUNKS = 3


def grad_kernel(transposed_ref, slope_ref, weight_ref, grad_ref, old_ref):
    rows = grad_ref.shape[0] // CHUNKS
    for i in range(CHUNKS):
        part = slice(i * rows, (i + 1) * rows)
        grad_ref[part, :] = jnp.dot(transposed_ref[part, :], slope_ref[...], preferred_element_type=f32)
        old_ref[part, :] = weight_ref[part, :]


def make_grad(transposed, slope, weight):
    return pl.pallas_call(
        grad_kernel,
        out_shape=(jax.ShapeDtypeStruct(weight.shape, f32), jax.ShapeDtypeStruct(weight.shape, bf16)),
        in_specs=[INSIDE] * 3,
        out_specs=(INSIDE,) * 2,
        compiler_params=pltpu.CompilerParams(vmem_limit_bytes=20 << 20),
    )(transposed, slope, weight)


def update_kernel(keep_ref, received_ref, grad_ref, old_ref, row_second_ref, seconds_ref, col_root_ref,
                  input_grad_ref, new_row_ref, new_weight_ref, root_ref, new_ref, sems):
    win, wout = old_ref.shape
    groups = win // 128
    rows = win // CHUNKS

    def store(i):
        part = pl.ds(i * rows, rows)
        return pltpu.make_async_copy(new_ref.at[part], new_weight_ref.at[part], sems.at[i])

    grads, sums, total, _ = decode([received_ref[...]])
    input_grad_ref[...] = (grads + keep_ref[:, :win]).astype(bf16)
    sums += keep_ref[:groups, win:]
    total += keep_ref[groups : groups + 1, win : win + 1]
    new_row = 0.999 * row_second_ref[...] + 0.001 * (sums / WOUT)
    new_row_ref[...] = new_row
    scale = 0.999 * (seconds_ref[...] / WIN) + 0.001 * (total / WOUT / WIN)
    root = 100.0 * jnp.sqrt(new_row / (scale * (1.0 - 0.999**ADAM_STEP)))
    for i in range(groups):
        root_ref[128 * i : 128 * (i + 1), :] = jnp.transpose(jnp.broadcast_to(root[i : i + 1], (128, 128)))

    for i in range(CHUNKS):
        part = slice(i * rows, (i + 1) * rows)
        root = root_ref[part, :]
        for j in range(0, wout, 128):
            bottom = root * col_root_ref[:, j : j + 128] + 1e-06
            change = grad_ref[part, j : j + 128] / bottom
            new_ref[part, j : j + 128] = (old_ref[part, j : j + 128].astype(f32) - change).astype(bf16)
        store(i).start()
    for i in range(CHUNKS):
        store(i).wait()


def update(keep, received, grad, weight, row_second, seconds, col_root):
    win, wout = weight.shape
    return pl.pallas_call(
        update_kernel,
        out_shape=(
            jax.ShapeDtypeStruct((keep.shape[0], win), bf16),
            jax.ShapeDtypeStruct((win // 128, 128), f32),
            jax.ShapeDtypeStruct((win, wout), bf16),
        ),
        in_specs=[INSIDE] * 7,
        out_specs=(INSIDE, INSIDE, OUTSIDE),
        scratch_shapes=[
            pltpu.VMEM((win, 128), f32),
            pltpu.VMEM((win, wout), bf16),
            pltpu.SemaphoreType.DMA((CHUNKS,)),
        ],
        compiler_params=pltpu.CompilerParams(vmem_limit_bytes=20 << 20),
    )(keep, received, grad, weight, row_second.reshape(-1, 128), seconds, col_root)


SWAP = ((0, 1), (1, 0))


def local(samples, cotangent, weight, row_second, col_second):
    own, win = samples.shape
    share, wout = cotangent.shape
    batch = own * COLS
    core, zh = lax.axis_index("core").astype(jnp.int32), lax.axis_index("zh").astype(jnp.int32)
    place = ((core * X + lax.axis_index("x")) * ZL + lax.axis_index("zl")).astype(jnp.int32)
    samples, core, zh, place, first = lax.optimization_barrier((samples, core, zh, place, core == 0))

    near = lax.all_gather(samples, "zh", axis=0, tiled=True)
    gathered = gather(near, "y", Y).reshape(X, ZL, CORE, share, win).transpose(2, 0, 1, 3, 4)
    mine = jnp.where(first, gathered[0], gathered[1]).reshape(batch // CORE, win)
    theirs = jnp.where(first, gathered[1], gathered[0]).reshape(batch // CORE, win)
    gathered = gathered.reshape(batch, win)

    def partial(rows):
        gram = lax.dot_general(rows, gathered, NT, preferred_element_type=f32)
        return jnp.concatenate([jnp.dot(rows, weight, preferred_element_type=f32), gram * GRAM_SCALE], axis=1)

    sums = lax.ppermute(partial(theirs).astype(f16), "core", SWAP).astype(f32) + partial(mine)
    for axis, size in (("x", X), ("zl", ZL)):
        blocks = sums.astype(f16).reshape(size, sums.shape[0] // size, sums.shape[1])
        sums = jnp.sum(exchange(blocks, axis).astype(f32), axis=0)

    packed = pack(place[None], sums, cotangent, row_second.reshape(-1, 128))
    for axis, size in (("zl", ZL), ("x", X)):
        packed = gather(packed, axis, size).reshape(packed.shape[0] * size, packed.shape[1])
    other = lax.ppermute(packed, "core", SWAP)

    message, seconds, slope, gram = make_message(core[None], packed, other, gathered, weight)
    message = exchange(message.astype(f16).reshape(Y, ZH, own, win + 128), "y").astype(f32)
    message, slope, gram, gathered = lax.optimization_barrier((message, slope, gram, gathered))
    keep, send = decoded(zh[None], message)
    received = lax.ppermute(send.astype(f16), "zh", SWAP).astype(f32)

    gram_high, gram_low = split(gram)
    mixed = jnp.dot(gram_high, slope, preferred_element_type=f32)
    mixed += jnp.dot(gram_low.astype(bf16), slope, preferred_element_type=f32)
    col_total = jnp.sum(slope.astype(f32) * mixed, axis=0) / GRAM_SCALE
    new_col = 0.999 * col_second + 0.001 * (col_total / WIN)
    grad, old = make_grad(gathered.T, slope, weight)
    input_grad, new_row, new_weight = update(
        keep, received, grad, old, row_second, seconds, jnp.sqrt(new_col)[None]
    )
    return (input_grad, new_weight, new_row.reshape(win), new_col)


def solution(mesh):
    fine = Mesh(mesh.devices.reshape(X, ZL, CORE, Y, ZH), ("x", "zl", "core", "y", "zh"))
    row, col = ("x", "zl", "core"), ("y", "zh")
    in_specs = (P(col, row), P(row, col), P(row, col), P(row), P(col))
    out_specs = (P(col, row), P(row, col), P(row), P(col))
    return jax.shard_map(local, mesh=fine, in_specs=in_specs, out_specs=out_specs, check_vma=False)
```

```python
import jax
import jax.numpy as jnp
from jax import lax
from jax.experimental import pallas as pl
from jax.experimental.pallas import tpu as pltpu
from jax.sharding import Mesh
from jax.sharding import PartitionSpec as P

WIN = 36864
WOUT = 24576
ADAM_STEP = 10
WEIGHT_MAX = 0.03125
GRAM_SCALE = 1.0 / 32.0

X, ZL, CORE, Y, ZH = 4, 6, 2, 8, 2
ROWS = X * ZL * CORE
COLS = Y * ZH
f32, f16, bf16 = jnp.float32, jnp.float16, jnp.bfloat16


def silu_slope(preact):
    sig = jax.nn.sigmoid(preact)
    return sig * (1.0 + preact * (1.0 - sig))


def exchange(blocks, axis):
    return lax.all_to_all(blocks, axis, 0, 0)


def gather(block, axis, size):
    return exchange(jnp.broadcast_to(block[None], (size,) + block.shape), axis)


def exponent(bound):
    return jnp.ceil(jnp.log2(jnp.maximum(bound, 1e-30))) - 15.0


def split(value):
    high = lax.reduce_precision(value, 8, 7)
    return high.astype(bf16), value - high


def whole(value):
    return jnp.sum(jnp.sum(value, axis=0, keepdims=True), axis=1, keepdims=True)


def encode(own, grad_exp, rows, total):
    row_exp = exponent(jnp.max(jnp.max(rows, axis=0, keepdims=True), axis=1, keepdims=True))
    total_exp = exponent(total)
    rows = rows * jnp.exp2(-row_exp)
    rows_high = rows.astype(bf16).astype(f32)
    total = total * jnp.exp2(-total_exp)
    total_high = total.astype(bf16).astype(f32)
    lanes = lax.broadcasted_iota(jnp.int32, (1, 128), 1)
    scalars = jnp.zeros((1, 128), f32)
    for i, value in enumerate((grad_exp, row_exp, total_exp, total_high, (total - total_high) * 256.0)):
        scalars = jnp.where(lanes == i, value, scalars)
    pad = jnp.zeros((own - 2 * rows.shape[0] - 1, 128), f32)
    return jnp.concatenate([rows_high, (rows - rows_high) * 256.0, scalars, pad], axis=0)


NT = (((1,), (1,)), ((), ()))


def halves(batch):
    return batch // 2 + batch // ROWS


def pack_kernel(place_ref, sums_ref, cotangent_ref, row_second_ref, packed_ref):
    share, wout = cotangent_ref.shape
    batch = sums_ref.shape[1] - wout
    side = packed_ref.shape[1] - wout
    count = halves(batch)
    packed_ref[:, :wout] = (cotangent_ref[...].astype(f32) * silu_slope(sums_ref[:, :wout])).astype(bf16)
    shift = lax.rem(batch - place_ref[0] * share, batch)
    gram = pltpu.roll(sums_ref[:, wout:], shift, 1)
    gram = jnp.concatenate([gram, jnp.zeros((share, side - batch), f32)], axis=1)
    high = gram.astype(bf16).astype(f32)
    low = pltpu.roll(gram - high, count, 1)
    lanes = lax.broadcasted_iota(jnp.int32, (share, side), 1)
    out = jnp.where(lanes < count, high, jnp.where(lanes < 2 * count, low, 0.0))
    rest = whole(row_second_ref[...])
    for i in range(3):
        part = rest.astype(bf16).astype(f32)
        rest = rest - part
        out = jnp.where(lanes == 2 * count + i, part, out)
    packed_ref[:, wout:] = out.astype(bf16)


def pack(place, sums, cotangent, row_second):
    share, wout = cotangent.shape
    width = wout + -(-(2 * halves(sums.shape[1] - wout) + 3) // 128) * 128
    return pl.pallas_call(
        pack_kernel,
        out_shape=jax.ShapeDtypeStruct((share, width), bf16),
        in_specs=[pl.BlockSpec(memory_space=pltpu.SMEM)] + [pl.BlockSpec(memory_space=pltpu.VMEM)] * 3,
        out_specs=pl.BlockSpec(memory_space=pltpu.VMEM),
        compiler_params=pltpu.CompilerParams(vmem_limit_bytes=16 << 20),
    )(place, sums, cotangent, row_second)


def message_kernel(core_ref, mine_ref, other_ref, samples_ref, weight_ref,
                   message_ref, seconds_ref, slope_ref, gram_ref, partial_ref):
    batch, win = samples_ref.shape
    wout = weight_ref.shape[1]
    own = batch // COLS
    share = batch // ROWS
    half = batch // CORE
    first = core_ref[0] == 0
    packed_half = []
    for i, (low, high) in enumerate(((mine_ref, other_ref), (other_ref, mine_ref))):
        both = jnp.where(first, low[...], high[...])
        slope_ref[i * half : (i + 1) * half, :] = both[:, :wout]
        packed_half.append(both[:, wout:].astype(f32))
    packed_half = jnp.concatenate(packed_half, axis=0)
    slope = slope_ref[...]
    partial_ref[...] = lax.dot_general(slope, weight_ref[...], NT, preferred_element_type=f32)
    count = halves(batch)
    lanes = lax.broadcasted_iota(jnp.int32, packed_half.shape, 1)
    there = (lanes >= 2 * count) & (lanes < 2 * count + 3)
    seconds_ref[...] = whole(jnp.where(there, packed_half, 0.0)) * (1.0 / share)
    lanes = lax.broadcasted_iota(jnp.int32, (share, batch), 1)
    times = jnp.where(lanes < share, 1.0, jnp.where(lanes < batch // 2, 2.0, jnp.where(lanes < count, 1.0, 0.0)))
    for place in range(ROWS):
        piece = packed_half[place * share : (place + 1) * share, :]
        piece = piece + pltpu.roll(piece, piece.shape[1] - count, 1)
        gram_ref[place * share : (place + 1) * share, :] = pltpu.roll(piece[:, :batch] * times, place * share, 1)
    gram = gram_ref[...]
    partial_ref[...] = lax.dot_general(slope, weight_ref[...], NT, preferred_element_type=f32)
    mixed = lax.dot_general(slope, slope, NT, preferred_element_type=f32)
    total = whole(mixed * gram) * (1.0 / GRAM_SCALE)
    mixed_high = mixed.astype(bf16)
    mixed_low = (mixed - mixed_high.astype(f32)).astype(bf16)
    samples = samples_ref[...]
    spread = jnp.dot(mixed_high, samples, preferred_element_type=f32)
    spread += jnp.dot(mixed_low, samples, preferred_element_type=f32)
    row_total = jnp.sum(samples.astype(f32) * spread, axis=0, keepdims=True)

    top = jnp.max(jnp.max(jnp.abs(slope), axis=0, keepdims=True).astype(f32), axis=1, keepdims=True)
    grad_exp = exponent(top * (WEIGHT_MAX * wout))
    rows = jnp.concatenate([row_total[:, 128 * i : 128 * (i + 1)] for i in range(win // 128)], axis=0)
    side = encode(own, grad_exp, rows, total)
    factor = jnp.exp2(-grad_exp)
    each = own // share
    for dest in range(COLS):
        blocks = []
        for block in range(dest * each, (dest + 1) * each):
            start = ((block % CORE) * (ROWS // CORE) + block // CORE) * share
            blocks.append(partial_ref[start : start + share, :])
        message_ref[dest, :, :win] = jnp.concatenate(blocks, axis=0) * factor
        message_ref[dest, :, win:] = side


INSIDE, OUTSIDE = pl.BlockSpec(memory_space=pltpu.VMEM), pl.BlockSpec(memory_space=pltpu.HBM)
SCALAR = pl.BlockSpec(memory_space=pltpu.SMEM)


def make_message(core, mine, other, samples, weight):
    batch, win = samples.shape
    return pl.pallas_call(
        message_kernel,
        out_shape=(
            jax.ShapeDtypeStruct((COLS, batch // COLS, win + 128), f32),
            jax.ShapeDtypeStruct((1, 1), f32),
            jax.ShapeDtypeStruct((batch, weight.shape[1]), bf16),
            jax.ShapeDtypeStruct((batch, batch), f32),
        ),
        in_specs=[SCALAR] + [INSIDE] * 4,
        out_specs=(INSIDE,) * 4,
        scratch_shapes=[pltpu.VMEM((batch, win), f32)],
        compiler_params=pltpu.CompilerParams(vmem_limit_bytes=20 << 20),
    )(core, mine, other, samples, weight)


def decode(pieces):
    own, width = pieces[0].shape
    win = width - 128
    groups = win // 128
    scalars = jnp.concatenate([piece[2 * groups : 2 * groups + 1, win:] for piece in pieces], axis=0)
    powers = jnp.exp2(scalars)
    grads = jnp.zeros((own, win), f32)
    sums = jnp.zeros((groups, 128), f32)
    for i, piece in enumerate(pieces):
        grads += piece[:, :win] * powers[i : i + 1, 0:1]
        side = piece[: 2 * groups, win:]
        sums += (side[:groups] + side[groups:] * (1.0 / 256.0)) * powers[i : i + 1, 1:2]
    total = whole((scalars[:, 3:4] + scalars[:, 4:5] * (1.0 / 256.0)) * powers[:, 2:3])
    return grads, sums, total, jnp.max(scalars[:, 0:1], axis=0, keepdims=True)


def decode_kernel(zh_ref, message_ref, keep_ref, send_ref):
    zh = zh_ref[0]
    grads, sums, total, _ = decode([message_ref[i, zh] for i in range(Y)])
    own, win = grads.shape
    keep_ref[:, :win] = grads
    lanes = lax.broadcasted_iota(jnp.int32, (1, 128), 1)
    rows = [sums, jnp.where(lanes == 0, total, 0.0), jnp.zeros((own - sums.shape[0] - 1, 128), f32)]
    keep_ref[:, win:] = jnp.concatenate(rows, axis=0)
    grads, sums, total, grad_exp = decode([message_ref[i, 1 - zh] for i in range(Y)])
    grad_exp += 3.0
    send_ref[:, :win] = grads * jnp.exp2(-grad_exp)
    send_ref[:, win:] = encode(own, grad_exp, sums, total)


def decoded(zh, message):
    return pl.pallas_call(
        decode_kernel,
        out_shape=(jax.ShapeDtypeStruct(message.shape[2:], f32),) * 2,
        in_specs=[SCALAR, INSIDE],
        out_specs=(INSIDE,) * 2,
        compiler_params=pltpu.CompilerParams(vmem_limit_bytes=12 << 20),
    )(zh, message)


CHUNKS = 3


def grad_kernel(samples_ref, slope_ref, gram_ref, col_second_ref, grad_ref, new_col_ref, col_root_ref):
    win, wout = grad_ref.shape
    rows = win // CHUNKS
    gram = gram_ref[...]
    gram_high = gram.astype(bf16)
    gram_low = (gram - gram_high.astype(f32)).astype(bf16)
    columns = wout // CHUNKS
    for i in range(CHUNKS):
        part = slice(i * columns, (i + 1) * columns)
        slope = slope_ref[:, part]
        mixed = jnp.dot(gram_high, slope, preferred_element_type=f32)
        mixed += jnp.dot(gram_low, slope, preferred_element_type=f32)
        col_total = jnp.sum(slope.astype(f32) * mixed, axis=0, keepdims=True) * (1.0 / GRAM_SCALE)
        lines = slice(i * columns // 128, (i + 1) * columns // 128)
        second = jnp.concatenate([col_second_ref[j : j + 1, :] for j in range(lines.start, lines.stop)], axis=1)
        new_col = 0.999 * second + 0.001 * (col_total / WIN)
        new_col_ref[lines, :] = jnp.concatenate([new_col[:, j : j + 128] for j in range(0, columns, 128)], axis=0)
        col_root_ref[:, part] = jnp.sqrt(new_col)
    for i in range(CHUNKS):
        part = slice(i * rows, (i + 1) * rows)
        grad_ref[part, :] = lax.dot_general(
            samples_ref[:, part], slope_ref[...], (((0,), (0,)), ((), ())), preferred_element_type=f32
        )


def make_grad(samples, slope, gram, col_second):
    shape = (samples.shape[1], slope.shape[1])
    return pl.pallas_call(
        grad_kernel,
        out_shape=(
            jax.ShapeDtypeStruct(shape, f32),
            jax.ShapeDtypeStruct(col_second.shape, f32),
            jax.ShapeDtypeStruct((1, shape[1]), f32),
        ),
        in_specs=[INSIDE] * 4,
        out_specs=(INSIDE,) * 3,
        compiler_params=pltpu.CompilerParams(vmem_limit_bytes=14 << 20),
    )(samples, slope, gram, col_second)


def update_kernel(keep_ref, received_ref, grad_ref, old_ref, row_second_ref, seconds_ref, col_root_ref,
                  input_grad_ref, new_row_ref, new_weight_ref, root_ref, new_ref, sems):
    win, wout = old_ref.shape
    groups = win // 128
    rows = win // CHUNKS

    def store(i):
        part = pl.ds(i * rows, rows)
        return pltpu.make_async_copy(new_ref.at[part], new_weight_ref.at[part], sems.at[i])

    grads, sums, total, _ = decode([received_ref[...]])
    input_grad_ref[...] = (grads + keep_ref[:, :win]).astype(bf16)
    sums += keep_ref[:groups, win:]
    total += keep_ref[groups : groups + 1, win : win + 1]
    new_row = 0.999 * row_second_ref[...] + 0.001 * (sums / WOUT)
    new_row_ref[...] = new_row
    scale = 0.999 * (seconds_ref[...] / WIN) + 0.001 * (total / WOUT / WIN)
    root = 100.0 * jnp.sqrt(new_row / (scale * (1.0 - 0.999**ADAM_STEP)))
    for i in range(groups):
        root_ref[128 * i : 128 * (i + 1), :] = jnp.transpose(jnp.broadcast_to(root[i : i + 1], (128, 128)))

    for i in range(CHUNKS):
        part = slice(i * rows, (i + 1) * rows)
        root = root_ref[part, :]
        for j in range(0, wout, 128):
            bottom = root * col_root_ref[:, j : j + 128] + 1e-06
            change = grad_ref[part, j : j + 128] / bottom
            new_ref[part, j : j + 128] = (old_ref[part, j : j + 128].astype(f32) - change).astype(bf16)
        store(i).start()
    for i in range(CHUNKS):
        store(i).wait()


def update(keep, received, grad, weight, row_second, seconds, col_root):
    win, wout = weight.shape
    return pl.pallas_call(
        update_kernel,
        out_shape=(
            jax.ShapeDtypeStruct((keep.shape[0], win), bf16),
            jax.ShapeDtypeStruct((win // 128, 128), f32),
            jax.ShapeDtypeStruct((win, wout), bf16),
        ),
        in_specs=[INSIDE] * 7,
        out_specs=(INSIDE, INSIDE, OUTSIDE),
        scratch_shapes=[
            pltpu.VMEM((win, 128), f32),
            pltpu.VMEM((win, wout), bf16),
            pltpu.SemaphoreType.DMA((CHUNKS,)),
        ],
        compiler_params=pltpu.CompilerParams(vmem_limit_bytes=14 << 20),
    )(keep, received, grad, weight, row_second.reshape(-1, 128), seconds, col_root)


SWAP = ((0, 1), (1, 0))


def local(samples, cotangent, weight, row_second, col_second):
    own, win = samples.shape
    share, wout = cotangent.shape
    batch = own * COLS
    core, zh = lax.axis_index("core").astype(jnp.int32), lax.axis_index("zh").astype(jnp.int32)
    place = ((core * X + lax.axis_index("x")) * ZL + lax.axis_index("zl")).astype(jnp.int32)
    samples, core, zh, place, first = lax.optimization_barrier((samples, core, zh, place, core == 0))

    near = lax.all_gather(samples, "zh", axis=0, tiled=True)
    gathered = gather(near, "y", Y).reshape(X, ZL, CORE, share, win).transpose(2, 0, 1, 3, 4)
    mine = jnp.where(first, gathered[0], gathered[1]).reshape(batch // CORE, win)
    theirs = jnp.where(first, gathered[1], gathered[0]).reshape(batch // CORE, win)
    gathered = gathered.reshape(batch, win)

    def partial(rows):
        gram = lax.dot_general(rows, gathered, NT, preferred_element_type=f32)
        return jnp.concatenate([jnp.dot(rows, weight, preferred_element_type=f32), gram * GRAM_SCALE], axis=1)

    sums = lax.ppermute(partial(theirs).astype(f16), "core", SWAP).astype(f32) + partial(mine)
    for axis, size in (("x", X), ("zl", ZL)):
        blocks = sums.astype(f16).reshape(size, sums.shape[0] // size, sums.shape[1])
        sums = jnp.sum(exchange(blocks, axis).astype(f32), axis=0)

    packed = pack(place[None], sums, cotangent, row_second.reshape(-1, 128))
    packed = gather(packed, "zl", ZL).reshape(share * ZL, packed.shape[1])
    packed = lax.all_gather(packed, "x", axis=0, tiled=True)
    other = lax.ppermute(packed, "core", SWAP)

    message, seconds, slope, gram = make_message(core[None], packed, other, gathered, weight)
    message = exchange(message.astype(f16).reshape(Y, ZH, own, win + 128), "y").astype(f32)
    message, slope, gram, gathered = lax.optimization_barrier((message, slope, gram, gathered))
    keep, send = decoded(zh[None], message)
    received = lax.ppermute(send.astype(f16), "zh", SWAP).astype(f32)

    grad, new_col, col_root = make_grad(gathered, slope, gram, col_second.reshape(-1, 128))
    input_grad, new_row, new_weight = update(
        keep, received, grad, weight, row_second, seconds, col_root
    )
    return (input_grad, new_weight, new_row.reshape(win), new_col.reshape(wout))


def solution(mesh):
    fine = Mesh(mesh.devices.reshape(X, ZL, CORE, Y, ZH), ("x", "zl", "core", "y", "zh"))
    row, col = ("x", "zl", "core"), ("y", "zh")
    in_specs = (P(col, row), P(row, col), P(row, col), P(row), P(col))
    out_specs = (P(col, row), P(row, col), P(row), P(col))
    return jax.shard_map(local, mesh=fine, in_specs=in_specs, out_specs=out_specs, check_vma=False)
```

```python
import functools

import jax
import jax.numpy as jnp
from jax import lax
from jax.experimental import pallas as pl
from jax.experimental.pallas import tpu as pltpu
from jax.sharding import Mesh
from jax.sharding import PartitionSpec as P

WIN = 36864
WOUT = 24576
ADAM_STEP = 10
WEIGHT_MAX = 0.03125
GRAM_SCALE = 1.0 / 32.0

X, ZL, CORE, Y, ZH = 4, 6, 2, 8, 2
ROWS = X * ZL * CORE
COLS = Y * ZH
f32, f16, bf16 = jnp.float32, jnp.float16, jnp.bfloat16


def silu_slope(preact):
    sig = jax.nn.sigmoid(preact)
    return sig * (1.0 + preact * (1.0 - sig))


def exchange(blocks, axis):
    return lax.all_to_all(blocks, axis, 0, 0)


def gather(block, axis, size):
    return exchange(jnp.broadcast_to(block[None], (size,) + block.shape), axis)


def exponent(bound):
    return jnp.ceil(jnp.log2(jnp.maximum(bound, 1e-30))) - 15.0


def split(value):
    high = lax.reduce_precision(value, 8, 7)
    return high.astype(bf16), value - high


def whole(value):
    return jnp.sum(jnp.sum(value, axis=0, keepdims=True), axis=1, keepdims=True)


SIDE = 16


def encode(grad_exp, rows, total):
    row_exp = exponent(jnp.max(jnp.max(rows, axis=0, keepdims=True), axis=1, keepdims=True))
    total_exp = exponent(total)
    rows = rows * jnp.exp2(-row_exp)
    rows_high = rows.astype(bf16).astype(f32)
    total = total * jnp.exp2(-total_exp)
    total_high = total.astype(bf16).astype(f32)
    lanes = lax.broadcasted_iota(jnp.int32, (1, 128), 1)
    scalars = jnp.zeros((1, 128), f32)
    for i, value in enumerate((grad_exp, row_exp, total_exp, total_high, (total - total_high) * 256.0)):
        scalars = jnp.where(lanes == i, value, scalars)
    pad = jnp.zeros((SIDE - 2 * rows.shape[0] - 1, 128), f32)
    return jnp.concatenate([rows_high, (rows - rows_high) * 256.0, scalars, pad], axis=0)


NT = (((1,), (1,)), ((), ()))


def halves(batch):
    return batch // 2 + batch // ROWS


def pack_kernel(place_ref, sums_ref, cotangent_ref, row_second_ref, packed_ref):
    share, wout = cotangent_ref.shape
    batch = sums_ref.shape[1] - wout
    side = packed_ref.shape[1] - wout
    count = halves(batch)
    packed_ref[:, :wout] = (cotangent_ref[...].astype(f32) * silu_slope(sums_ref[:, :wout])).astype(bf16)
    shift = lax.rem(batch - place_ref[0] * share, batch)
    gram = pltpu.roll(sums_ref[:, wout:], shift, 1)
    gram = jnp.concatenate([gram, jnp.zeros((share, side - batch), f32)], axis=1)
    high = gram.astype(bf16).astype(f32)
    low = pltpu.roll(gram - high, count, 1)
    lanes = lax.broadcasted_iota(jnp.int32, (share, side), 1)
    out = jnp.where(lanes < count, high, jnp.where(lanes < 2 * count, low, 0.0))
    rest = whole(row_second_ref[...])
    for i in range(3):
        part = rest.astype(bf16).astype(f32)
        rest = rest - part
        out = jnp.where(lanes == 2 * count + i, part, out)
    packed_ref[:, wout:] = out.astype(bf16)


def pack(place, sums, cotangent, row_second):
    share, wout = cotangent.shape
    width = wout + -(-(2 * halves(sums.shape[1] - wout) + 3) // 128) * 128
    return pl.pallas_call(
        pack_kernel,
        out_shape=jax.ShapeDtypeStruct((share, width), bf16),
        in_specs=[pl.BlockSpec(memory_space=pltpu.SMEM)] + [pl.BlockSpec(memory_space=pltpu.VMEM)] * 3,
        out_specs=pl.BlockSpec(memory_space=pltpu.VMEM),
        compiler_params=pltpu.CompilerParams(vmem_limit_bytes=16 << 20),
    )(place, sums, cotangent, row_second)


def message_kernel(core_ref, mine_ref, other_ref, samples_ref, weight_ref,
                   message_ref, seconds_ref, slope_ref, gram_ref, partial_ref):
    batch, win = samples_ref.shape
    wout = weight_ref.shape[1]
    own = batch // COLS
    share = batch // ROWS
    half = batch // CORE
    first = core_ref[0] == 0
    packed_half = []
    for i, (low, high) in enumerate(((mine_ref, other_ref), (other_ref, mine_ref))):
        both = jnp.where(first, low[...], high[...])
        slope_ref[i * half : (i + 1) * half, :] = both[:, :wout]
        packed_half.append(both[:, wout:].astype(f32))
    packed_half = jnp.concatenate(packed_half, axis=0)
    slope = slope_ref[...]
    partial_ref[...] = lax.dot_general(slope, weight_ref[...], NT, preferred_element_type=f32)
    count = halves(batch)
    lanes = lax.broadcasted_iota(jnp.int32, packed_half.shape, 1)
    there = (lanes >= 2 * count) & (lanes < 2 * count + 3)
    seconds_ref[...] = whole(jnp.where(there, packed_half, 0.0)) * (1.0 / share)
    lanes = lax.broadcasted_iota(jnp.int32, (share, batch), 1)
    times = jnp.where(lanes < share, 1.0, jnp.where(lanes < batch // 2, 2.0, jnp.where(lanes < count, 1.0, 0.0)))
    for place in range(ROWS):
        piece = packed_half[place * share : (place + 1) * share, :]
        piece = piece + pltpu.roll(piece, piece.shape[1] - count, 1)
        gram_ref[place * share : (place + 1) * share, :] = pltpu.roll(piece[:, :batch] * times, place * share, 1)
    gram = gram_ref[...]
    partial_ref[...] = lax.dot_general(slope, weight_ref[...], NT, preferred_element_type=f32)
    mixed = lax.dot_general(slope, slope, NT, preferred_element_type=f32)
    total = whole(mixed * gram) * (1.0 / GRAM_SCALE)
    mixed_high = mixed.astype(bf16)
    mixed_low = (mixed - mixed_high.astype(f32)).astype(bf16)
    samples = samples_ref[...]
    spread = jnp.dot(mixed_high, samples, preferred_element_type=f32)
    spread += jnp.dot(mixed_low, samples, preferred_element_type=f32)
    row_total = jnp.sum(samples.astype(f32) * spread, axis=0, keepdims=True)

    top = jnp.max(jnp.max(jnp.abs(slope), axis=0, keepdims=True).astype(f32), axis=1, keepdims=True)
    grad_exp = exponent(top * (WEIGHT_MAX * wout))
    rows = jnp.concatenate([row_total[:, 128 * i : 128 * (i + 1)] for i in range(win // 128)], axis=0)
    side = encode(grad_exp, rows, total)
    factor = jnp.exp2(-grad_exp)
    each = own // share
    for dest in range(COLS):
        blocks = []
        for block in range(dest * each, (dest + 1) * each):
            start = ((block % CORE) * (ROWS // CORE) + block // CORE) * share
            blocks.append(partial_ref[start : start + share, :])
        grads = jnp.concatenate(blocks, axis=0) * factor
        for i in range(win // 128):
            start = (dest % ZH * (win // 128) + i) * own
            message_ref[dest // ZH, start : start + own, :] = grads[:, 128 * i : 128 * (i + 1)]
    for y in range(Y):
        message_ref[y, message_ref.shape[1] - SIDE :, :] = side


INSIDE, OUTSIDE = pl.BlockSpec(memory_space=pltpu.VMEM), pl.BlockSpec(memory_space=pltpu.HBM)
SCALAR = pl.BlockSpec(memory_space=pltpu.SMEM)


def make_message(core, mine, other, samples, weight):
    batch, win = samples.shape
    return pl.pallas_call(
        message_kernel,
        out_shape=(
            jax.ShapeDtypeStruct((Y, ZH * (batch // COLS) * (win // 128) + SIDE, 128), f32),
            jax.ShapeDtypeStruct((1, 1), f32),
            jax.ShapeDtypeStruct((batch, weight.shape[1]), bf16),
            jax.ShapeDtypeStruct((batch, batch), f32),
        ),
        in_specs=[SCALAR] + [INSIDE] * 4,
        out_specs=(INSIDE,) * 4,
        scratch_shapes=[pltpu.VMEM((batch, win), f32)],
        compiler_params=pltpu.CompilerParams(vmem_limit_bytes=20 << 20),
    )(core, mine, other, samples, weight)


def decode(sides, groups):
    scalars = jnp.concatenate([side[2 * groups : 2 * groups + 1, :] for side in sides], axis=0)
    powers = jnp.exp2(scalars)
    sums = jnp.zeros((groups, 128), f32)
    for i, side in enumerate(sides):
        sums += (side[:groups] + side[groups : 2 * groups] * (1.0 / 256.0)) * powers[i : i + 1, 1:2]
    total = whole((scalars[:, 3:4] + scalars[:, 4:5] * (1.0 / 256.0)) * powers[:, 2:3])
    factors = [powers[i : i + 1, 0:1] for i in range(len(sides))]
    return factors, sums, total, jnp.max(scalars[:, 0:1], axis=0, keepdims=True)


def decode_kernel(groups, zh_ref, message_ref, keep_ref, send_ref):
    zh = zh_ref[0]
    size = keep_ref.shape[0] - SIDE
    factors, sums, total, grad_exp = decode([message_ref[i, ZH * size :, :] for i in range(Y)], groups)

    def grads(half):
        rows = pl.ds(pl.multiple_of(half * size, 8), size)
        return sum(message_ref[i, rows, :] * factors[i] for i in range(Y))

    lanes = lax.broadcasted_iota(jnp.int32, (1, 128), 1)
    rows = [sums, jnp.where(lanes == 0, total, 0.0), jnp.zeros((SIDE - groups - 1, 128), f32)]
    keep_ref[:size, :] = grads(zh)
    keep_ref[size:, :] = jnp.concatenate(rows, axis=0)
    grad_exp += 3.0
    send_ref[:size, :] = grads(1 - zh) * jnp.exp2(-grad_exp)
    send_ref[size:, :] = encode(grad_exp, sums, total)


def decoded(zh, message, groups):
    size = (message.shape[1] - SIDE) // ZH + SIDE
    return pl.pallas_call(
        functools.partial(decode_kernel, groups),
        out_shape=(jax.ShapeDtypeStruct((size, 128), f32),) * 2,
        in_specs=[SCALAR, INSIDE],
        out_specs=(INSIDE,) * 2,
        compiler_params=pltpu.CompilerParams(vmem_limit_bytes=12 << 20),
    )(zh, message)


CHUNKS = 3


def grad_kernel(samples_ref, slope_ref, gram_ref, col_second_ref, grad_ref, new_col_ref, col_root_ref):
    win, wout = grad_ref.shape
    rows = win // CHUNKS
    gram = gram_ref[...]
    gram_high = gram.astype(bf16)
    gram_low = (gram - gram_high.astype(f32)).astype(bf16)
    columns = wout // CHUNKS
    for i in range(CHUNKS):
        part = slice(i * columns, (i + 1) * columns)
        slope = slope_ref[:, part]
        mixed = jnp.dot(gram_high, slope, preferred_element_type=f32)
        mixed += jnp.dot(gram_low, slope, preferred_element_type=f32)
        col_total = jnp.sum(slope.astype(f32) * mixed, axis=0, keepdims=True) * (1.0 / GRAM_SCALE)
        lines = slice(i * columns // 128, (i + 1) * columns // 128)
        second = jnp.concatenate([col_second_ref[j : j + 1, :] for j in range(lines.start, lines.stop)], axis=1)
        new_col = 0.999 * second + 0.001 * (col_total / WIN)
        new_col_ref[lines, :] = jnp.concatenate([new_col[:, j : j + 128] for j in range(0, columns, 128)], axis=0)
        col_root_ref[:, part] = jnp.sqrt(new_col)
    for i in range(CHUNKS):
        part = slice(i * rows, (i + 1) * rows)
        grad_ref[part, :] = lax.dot_general(
            samples_ref[:, part], slope_ref[...], (((0,), (0,)), ((), ())), preferred_element_type=f32
        )


def make_grad(samples, slope, gram, col_second):
    shape = (samples.shape[1], slope.shape[1])
    return pl.pallas_call(
        grad_kernel,
        out_shape=(
            jax.ShapeDtypeStruct(shape, f32),
            jax.ShapeDtypeStruct(col_second.shape, f32),
            jax.ShapeDtypeStruct((1, shape[1]), f32),
        ),
        in_specs=[INSIDE] * 4,
        out_specs=(INSIDE,) * 3,
        compiler_params=pltpu.CompilerParams(vmem_limit_bytes=14 << 20),
    )(samples, slope, gram, col_second)


def update_kernel(keep_ref, received_ref, grad_ref, old_ref, row_second_ref, seconds_ref, col_root_ref,
                  input_grad_ref, new_row_ref, new_weight_ref, root_ref, new_ref, sems):
    win, wout = old_ref.shape
    groups = win // 128
    rows = win // CHUNKS

    def store(i):
        part = pl.ds(i * rows, rows)
        return pltpu.make_async_copy(new_ref.at[part], new_weight_ref.at[part], sems.at[i])

    own = input_grad_ref.shape[0]
    size = own * groups
    factors, sums, total, _ = decode([received_ref[size:, :]], groups)
    for i in range(groups):
        part = slice(i * own, (i + 1) * own)
        grads = received_ref[part, :] * factors[0] + keep_ref[part, :]
        input_grad_ref[:, 128 * i : 128 * (i + 1)] = grads.astype(bf16)
    sums += keep_ref[size : size + groups, :]
    total += keep_ref[size + groups : size + groups + 1, :1]
    new_row = 0.999 * row_second_ref[...] + 0.001 * (sums / WOUT)
    new_row_ref[...] = new_row
    scale = 0.999 * (seconds_ref[...] / WIN) + 0.001 * (total / WOUT / WIN)
    root = 100.0 * jnp.sqrt(new_row / (scale * (1.0 - 0.999**ADAM_STEP)))
    for i in range(groups):
        root_ref[128 * i : 128 * (i + 1), :] = jnp.transpose(jnp.broadcast_to(root[i : i + 1], (128, 128)))

    for i in range(CHUNKS):
        part = slice(i * rows, (i + 1) * rows)
        root = root_ref[part, :]
        for j in range(0, wout, 128):
            bottom = root * col_root_ref[:, j : j + 128] + 1e-06
            change = grad_ref[part, j : j + 128] / bottom
            new_ref[part, j : j + 128] = (old_ref[part, j : j + 128].astype(f32) - change).astype(bf16)
        store(i).start()
    for i in range(CHUNKS):
        store(i).wait()


def update(own, keep, received, grad, weight, row_second, seconds, col_root):
    win, wout = weight.shape
    return pl.pallas_call(
        update_kernel,
        out_shape=(
            jax.ShapeDtypeStruct((own, win), bf16),
            jax.ShapeDtypeStruct((win // 128, 128), f32),
            jax.ShapeDtypeStruct((win, wout), bf16),
        ),
        in_specs=[INSIDE] * 7,
        out_specs=(INSIDE, INSIDE, OUTSIDE),
        scratch_shapes=[
            pltpu.VMEM((win, 128), f32),
            pltpu.VMEM((win, wout), bf16),
            pltpu.SemaphoreType.DMA((CHUNKS,)),
        ],
        compiler_params=pltpu.CompilerParams(vmem_limit_bytes=14 << 20),
    )(keep, received, grad, weight, row_second.reshape(-1, 128), seconds, col_root)


SWAP = ((0, 1), (1, 0))


def local(samples, cotangent, weight, row_second, col_second):
    own, win = samples.shape
    share, wout = cotangent.shape
    batch = own * COLS
    core, zh = lax.axis_index("core").astype(jnp.int32), lax.axis_index("zh").astype(jnp.int32)
    place = ((core * X + lax.axis_index("x")) * ZL + lax.axis_index("zl")).astype(jnp.int32)
    samples, core, zh, place, first = lax.optimization_barrier((samples, core, zh, place, core == 0))

    near = lax.all_gather(samples, "zh", axis=0, tiled=True)
    gathered = gather(near, "y", Y).reshape(X, ZL, CORE, share, win).transpose(2, 0, 1, 3, 4)
    mine = jnp.where(first, gathered[0], gathered[1]).reshape(batch // CORE, win)
    theirs = jnp.where(first, gathered[1], gathered[0]).reshape(batch // CORE, win)
    gathered = gathered.reshape(batch, win)

    def partial(rows):
        gram = lax.dot_general(rows, gathered, NT, preferred_element_type=f32)
        return jnp.concatenate([jnp.dot(rows, weight, preferred_element_type=f32), gram * GRAM_SCALE], axis=1)

    sums = lax.ppermute(partial(theirs).astype(f16), "core", SWAP).astype(f32) + partial(mine)
    for axis, size in (("x", X), ("zl", ZL)):
        blocks = sums.astype(f16).reshape(size, sums.shape[0] // size, sums.shape[1])
        sums = jnp.sum(exchange(blocks, axis).astype(f32), axis=0)

    packed = pack(place[None], sums, cotangent, row_second.reshape(-1, 128))
    for axis, size in (("zl", ZL), ("x", X)):
        packed = gather(packed, axis, size).reshape(packed.shape[0] * size, packed.shape[1])
    other = lax.ppermute(packed, "core", SWAP)

    message, seconds, slope, gram = make_message(core[None], packed, other, gathered, weight)
    message = exchange(message.astype(f16), "y").astype(f32)
    message, slope, gram, gathered = lax.optimization_barrier((message, slope, gram, gathered))
    keep, send = decoded(zh[None], message, win // 128)
    received = lax.ppermute(send.astype(f16), "zh", SWAP).astype(f32)

    grad, new_col, col_root = make_grad(gathered, slope, gram, col_second.reshape(-1, 128))
    input_grad, new_row, new_weight = update(
        own, keep, received, grad, weight, row_second, seconds, col_root
    )
    return (input_grad, new_weight, new_row.reshape(win), new_col.reshape(wout))


def solution(mesh):
    fine = Mesh(mesh.devices.reshape(X, ZL, CORE, Y, ZH), ("x", "zl", "core", "y", "zh"))
    row, col = ("x", "zl", "core"), ("y", "zh")
    in_specs = (P(col, row), P(row, col), P(row, col), P(row), P(col))
    out_specs = (P(col, row), P(row, col), P(row), P(col))
    return jax.shard_map(local, mesh=fine, in_specs=in_specs, out_specs=out_specs, check_vma=False)
```

```python
import functools

import jax
import jax.numpy as jnp
from jax import lax
from jax.experimental import pallas as pl
from jax.experimental.pallas import tpu as pltpu
from jax.sharding import Mesh
from jax.sharding import PartitionSpec as P

WIN = 36864
WOUT = 24576
ADAM_STEP = 10
WEIGHT_MAX = 0.03125
GRAM_SCALE = 1.0 / 32.0

X, ZL, CORE, Y, ZH = 4, 6, 2, 8, 2
ROWS = X * ZL * CORE
COLS = Y * ZH
f32, f16, bf16 = jnp.float32, jnp.float16, jnp.bfloat16


def silu_slope(preact):
    sig = jax.nn.sigmoid(preact)
    return sig * (1.0 + preact * (1.0 - sig))


def exchange(blocks, axis):
    return lax.all_to_all(blocks, axis, 0, 0)


def gather(block, axis, size):
    return exchange(jnp.broadcast_to(block[None], (size,) + block.shape), axis)


def exponent(bound):
    return jnp.ceil(jnp.log2(jnp.maximum(bound, 1e-30))) - 15.0


def split(value):
    high = lax.reduce_precision(value, 8, 7)
    return high.astype(bf16), value - high


def whole(value):
    return jnp.sum(jnp.sum(value, axis=0, keepdims=True), axis=1, keepdims=True)


SIDE = 16


def encode(grad_exp, rows, total):
    row_exp = exponent(jnp.max(jnp.max(rows, axis=0, keepdims=True), axis=1, keepdims=True))
    total_exp = exponent(total)
    rows = rows * jnp.exp2(-row_exp)
    rows_high = rows.astype(bf16).astype(f32)
    total = total * jnp.exp2(-total_exp)
    total_high = total.astype(bf16).astype(f32)
    lanes = lax.broadcasted_iota(jnp.int32, (1, 128), 1)
    scalars = jnp.zeros((1, 128), f32)
    for i, value in enumerate((grad_exp, row_exp, total_exp, total_high, (total - total_high) * 256.0)):
        scalars = jnp.where(lanes == i, value, scalars)
    pad = jnp.zeros((SIDE - 2 * rows.shape[0] - 1, 128), f32)
    return jnp.concatenate([rows_high, (rows - rows_high) * 256.0, scalars, pad], axis=0)


NT = (((1,), (1,)), ((), ()))


def halves(batch):
    return batch // 2 + batch // ROWS


def pack_kernel(place_ref, sums_ref, cotangent_ref, row_second_ref, packed_ref):
    share, wout = cotangent_ref.shape
    batch = sums_ref.shape[1] - wout
    side = packed_ref.shape[1] - wout
    count = halves(batch)
    packed_ref[:, :wout] = (cotangent_ref[...].astype(f32) * silu_slope(sums_ref[:, :wout])).astype(bf16)
    shift = lax.rem(batch - place_ref[0] * share, batch)
    gram = pltpu.roll(sums_ref[:, wout:], shift, 1)
    gram = jnp.concatenate([gram, jnp.zeros((share, side - batch), f32)], axis=1)
    high = gram.astype(bf16).astype(f32)
    low = pltpu.roll(gram - high, count, 1)
    lanes = lax.broadcasted_iota(jnp.int32, (share, side), 1)
    out = jnp.where(lanes < count, high, jnp.where(lanes < 2 * count, low, 0.0))
    rest = whole(row_second_ref[...])
    for i in range(3):
        part = rest.astype(bf16).astype(f32)
        rest = rest - part
        out = jnp.where(lanes == 2 * count + i, part, out)
    packed_ref[:, wout:] = out.astype(bf16)


def pack(place, sums, cotangent, row_second):
    share, wout = cotangent.shape
    width = wout + -(-(2 * halves(sums.shape[1] - wout) + 3) // 128) * 128
    return pl.pallas_call(
        pack_kernel,
        out_shape=jax.ShapeDtypeStruct((share, width), bf16),
        in_specs=[pl.BlockSpec(memory_space=pltpu.SMEM)] + [pl.BlockSpec(memory_space=pltpu.VMEM)] * 3,
        out_specs=pl.BlockSpec(memory_space=pltpu.VMEM),
        compiler_params=pltpu.CompilerParams(vmem_limit_bytes=16 << 20),
    )(place, sums, cotangent, row_second)


def early_kernel(mine_ref, weight_ref, early_ref):
    slope = mine_ref[:, : weight_ref.shape[1]]
    early_ref[...] = lax.dot_general(slope, weight_ref[...], NT, preferred_element_type=f32)


def make_early(mine, weight):
    rows, (win, wout) = mine.shape[0], weight.shape
    return pl.pallas_call(
        early_kernel,
        out_shape=jax.ShapeDtypeStruct((rows, win), f32),
        in_specs=[INSIDE] * 2,
        out_specs=INSIDE,
        compiler_params=pltpu.CompilerParams(vmem_limit_bytes=14 << 20),
        cost_estimate=pl.CostEstimate(flops=2 * rows * win * wout, bytes_accessed=2 * win * wout, transcendentals=0),
    )(mine, weight)


def message_kernel(core_ref, early_ref, mine_ref, other_ref, samples_ref, weight_ref,
                   message_ref, seconds_ref, slope_ref, gram_ref, partial_ref):
    batch, win = samples_ref.shape
    wout = weight_ref.shape[1]
    own = batch // COLS
    share = batch // ROWS
    half = batch // CORE
    first = core_ref[0] == 0
    packed_half = []
    for i, (low, high) in enumerate(((mine_ref, other_ref), (other_ref, mine_ref))):
        both = jnp.where(first, low[...], high[...])
        slope_ref[i * half : (i + 1) * half, :] = both[:, :wout]
        packed_half.append(both[:, wout:].astype(f32))
    packed_half = jnp.concatenate(packed_half, axis=0)
    slope = slope_ref[...]
    partial_ref[pl.ds(pl.multiple_of(core_ref[0] * half, 8), half), :] = early_ref[...]
    partial_ref[pl.ds(pl.multiple_of((1 - core_ref[0]) * half, 8), half), :] = lax.dot_general(
        other_ref[:, :wout], weight_ref[...], NT, preferred_element_type=f32
    )
    count = halves(batch)
    lanes = lax.broadcasted_iota(jnp.int32, packed_half.shape, 1)
    there = (lanes >= 2 * count) & (lanes < 2 * count + 3)
    seconds_ref[...] = whole(jnp.where(there, packed_half, 0.0)) * (1.0 / share)
    lanes = lax.broadcasted_iota(jnp.int32, (share, batch), 1)
    times = jnp.where(lanes < share, 1.0, jnp.where(lanes < batch // 2, 2.0, jnp.where(lanes < count, 1.0, 0.0)))
    for place in range(ROWS):
        piece = packed_half[place * share : (place + 1) * share, :]
        piece = piece + pltpu.roll(piece, piece.shape[1] - count, 1)
        gram_ref[place * share : (place + 1) * share, :] = pltpu.roll(piece[:, :batch] * times, place * share, 1)
    gram = gram_ref[...]
    mixed = lax.dot_general(slope, slope, NT, preferred_element_type=f32)
    total = whole(mixed * gram) * (1.0 / GRAM_SCALE)
    mixed_high = mixed.astype(bf16)
    mixed_low = (mixed - mixed_high.astype(f32)).astype(bf16)
    samples = samples_ref[...]
    spread = jnp.dot(mixed_high, samples, preferred_element_type=f32)
    spread += jnp.dot(mixed_low, samples, preferred_element_type=f32)
    row_total = jnp.sum(samples.astype(f32) * spread, axis=0, keepdims=True)

    top = jnp.max(jnp.max(jnp.abs(slope), axis=0, keepdims=True).astype(f32), axis=1, keepdims=True)
    grad_exp = exponent(top * (WEIGHT_MAX * wout))
    rows = jnp.concatenate([row_total[:, 128 * i : 128 * (i + 1)] for i in range(win // 128)], axis=0)
    side = encode(grad_exp, rows, total)
    factor = jnp.exp2(-grad_exp)
    each = own // share
    for dest in range(COLS):
        blocks = []
        for block in range(dest * each, (dest + 1) * each):
            start = ((block % CORE) * (ROWS // CORE) + block // CORE) * share
            blocks.append(partial_ref[start : start + share, :])
        grads = jnp.concatenate(blocks, axis=0) * factor
        for i in range(win // 128):
            start = (dest % ZH * (win // 128) + i) * own
            message_ref[dest // ZH, start : start + own, :] = grads[:, 128 * i : 128 * (i + 1)]
    for y in range(Y):
        message_ref[y, message_ref.shape[1] - SIDE :, :] = side


INSIDE, OUTSIDE = pl.BlockSpec(memory_space=pltpu.VMEM), pl.BlockSpec(memory_space=pltpu.HBM)
SCALAR = pl.BlockSpec(memory_space=pltpu.SMEM)


def make_message(core, early, mine, other, samples, weight):
    batch, win = samples.shape
    return pl.pallas_call(
        message_kernel,
        out_shape=(
            jax.ShapeDtypeStruct((Y, ZH * (batch // COLS) * (win // 128) + SIDE, 128), f32),
            jax.ShapeDtypeStruct((1, 1), f32),
            jax.ShapeDtypeStruct((batch, weight.shape[1]), bf16),
            jax.ShapeDtypeStruct((batch, batch), f32),
        ),
        in_specs=[SCALAR] + [INSIDE] * 5,
        out_specs=(INSIDE,) * 4,
        scratch_shapes=[pltpu.VMEM((batch, win), f32)],
        compiler_params=pltpu.CompilerParams(vmem_limit_bytes=20 << 20),
    )(core, early, mine, other, samples, weight)


def decode(sides, groups):
    scalars = jnp.concatenate([side[2 * groups : 2 * groups + 1, :] for side in sides], axis=0)
    powers = jnp.exp2(scalars)
    sums = jnp.zeros((groups, 128), f32)
    for i, side in enumerate(sides):
        sums += (side[:groups] + side[groups : 2 * groups] * (1.0 / 256.0)) * powers[i : i + 1, 1:2]
    total = whole((scalars[:, 3:4] + scalars[:, 4:5] * (1.0 / 256.0)) * powers[:, 2:3])
    factors = [powers[i : i + 1, 0:1] for i in range(len(sides))]
    return factors, sums, total, jnp.max(scalars[:, 0:1], axis=0, keepdims=True)


def decode_kernel(groups, zh_ref, message_ref, keep_ref, send_ref):
    zh = zh_ref[0]
    size = keep_ref.shape[0] - SIDE
    factors, sums, total, grad_exp = decode([message_ref[i, ZH * size :, :] for i in range(Y)], groups)

    def grads(half):
        rows = pl.ds(pl.multiple_of(half * size, 8), size)
        return sum(message_ref[i, rows, :] * factors[i] for i in range(Y))

    lanes = lax.broadcasted_iota(jnp.int32, (1, 128), 1)
    rows = [sums, jnp.where(lanes == 0, total, 0.0), jnp.zeros((SIDE - groups - 1, 128), f32)]
    keep_ref[:size, :] = grads(zh)
    keep_ref[size:, :] = jnp.concatenate(rows, axis=0)
    grad_exp += 3.0
    send_ref[:size, :] = grads(1 - zh) * jnp.exp2(-grad_exp)
    send_ref[size:, :] = encode(grad_exp, sums, total)


def decoded(zh, message, groups):
    size = (message.shape[1] - SIDE) // ZH + SIDE
    return pl.pallas_call(
        functools.partial(decode_kernel, groups),
        out_shape=(jax.ShapeDtypeStruct((size, 128), f32),) * 2,
        in_specs=[SCALAR, INSIDE],
        out_specs=(INSIDE,) * 2,
        compiler_params=pltpu.CompilerParams(vmem_limit_bytes=12 << 20),
    )(zh, message)


CHUNKS = 3


def grad_kernel(samples_ref, slope_ref, gram_ref, col_second_ref, grad_ref, new_col_ref, col_root_ref):
    win, wout = grad_ref.shape
    rows = win // CHUNKS
    gram = gram_ref[...]
    gram_high = gram.astype(bf16)
    gram_low = (gram - gram_high.astype(f32)).astype(bf16)
    columns = wout // CHUNKS
    for i in range(CHUNKS):
        part = slice(i * columns, (i + 1) * columns)
        slope = slope_ref[:, part]
        mixed = jnp.dot(gram_high, slope, preferred_element_type=f32)
        mixed += jnp.dot(gram_low, slope, preferred_element_type=f32)
        col_total = jnp.sum(slope.astype(f32) * mixed, axis=0, keepdims=True) * (1.0 / GRAM_SCALE)
        lines = slice(i * columns // 128, (i + 1) * columns // 128)
        second = jnp.concatenate([col_second_ref[j : j + 1, :] for j in range(lines.start, lines.stop)], axis=1)
        new_col = 0.999 * second + 0.001 * (col_total / WIN)
        new_col_ref[lines, :] = jnp.concatenate([new_col[:, j : j + 128] for j in range(0, columns, 128)], axis=0)
        col_root_ref[:, part] = jnp.sqrt(new_col)
    for i in range(CHUNKS):
        part = slice(i * rows, (i + 1) * rows)
        grad_ref[part, :] = lax.dot_general(
            samples_ref[:, part], slope_ref[...], (((0,), (0,)), ((), ())), preferred_element_type=f32
        )


def make_grad(samples, slope, gram, col_second):
    shape = (samples.shape[1], slope.shape[1])
    return pl.pallas_call(
        grad_kernel,
        out_shape=(
            jax.ShapeDtypeStruct(shape, f32),
            jax.ShapeDtypeStruct(col_second.shape, f32),
            jax.ShapeDtypeStruct((1, shape[1]), f32),
        ),
        in_specs=[INSIDE] * 4,
        out_specs=(INSIDE,) * 3,
        compiler_params=pltpu.CompilerParams(vmem_limit_bytes=14 << 20),
    )(samples, slope, gram, col_second)


def update_kernel(keep_ref, received_ref, grad_ref, old_ref, row_second_ref, seconds_ref, col_root_ref,
                  input_grad_ref, new_row_ref, new_weight_ref, root_ref, new_ref, sems):
    win, wout = old_ref.shape
    groups = win // 128
    rows = win // CHUNKS

    def store(i):
        part = pl.ds(i * rows, rows)
        return pltpu.make_async_copy(new_ref.at[part], new_weight_ref.at[part], sems.at[i])

    own = input_grad_ref.shape[0]
    size = own * groups
    factors, sums, total, _ = decode([received_ref[size:, :]], groups)
    for i in range(groups):
        part = slice(i * own, (i + 1) * own)
        grads = received_ref[part, :] * factors[0] + keep_ref[part, :]
        input_grad_ref[:, 128 * i : 128 * (i + 1)] = grads.astype(bf16)
    sums += keep_ref[size : size + groups, :]
    total += keep_ref[size + groups : size + groups + 1, :1]
    new_row = 0.999 * row_second_ref[...] + 0.001 * (sums / WOUT)
    new_row_ref[...] = new_row
    scale = 0.999 * (seconds_ref[...] / WIN) + 0.001 * (total / WOUT / WIN)
    root = 100.0 * jnp.sqrt(new_row / (scale * (1.0 - 0.999**ADAM_STEP)))
    for i in range(groups):
        root_ref[128 * i : 128 * (i + 1), :] = jnp.transpose(jnp.broadcast_to(root[i : i + 1], (128, 128)))

    for i in range(CHUNKS):
        part = slice(i * rows, (i + 1) * rows)
        root = root_ref[part, :]
        for j in range(0, wout, 128):
            bottom = root * col_root_ref[:, j : j + 128] + 1e-06
            change = grad_ref[part, j : j + 128] / bottom
            new_ref[part, j : j + 128] = (old_ref[part, j : j + 128].astype(f32) - change).astype(bf16)
        store(i).start()
    for i in range(CHUNKS):
        store(i).wait()


def update(own, keep, received, grad, weight, row_second, seconds, col_root):
    win, wout = weight.shape
    return pl.pallas_call(
        update_kernel,
        out_shape=(
            jax.ShapeDtypeStruct((own, win), bf16),
            jax.ShapeDtypeStruct((win // 128, 128), f32),
            jax.ShapeDtypeStruct((win, wout), bf16),
        ),
        in_specs=[INSIDE] * 7,
        out_specs=(INSIDE, INSIDE, OUTSIDE),
        scratch_shapes=[
            pltpu.VMEM((win, 128), f32),
            pltpu.VMEM((win, wout), bf16),
            pltpu.SemaphoreType.DMA((CHUNKS,)),
        ],
        compiler_params=pltpu.CompilerParams(vmem_limit_bytes=14 << 20),
    )(keep, received, grad, weight, row_second.reshape(-1, 128), seconds, col_root)


SWAP = ((0, 1), (1, 0))


def local(samples, cotangent, weight, row_second, col_second):
    own, win = samples.shape
    share, wout = cotangent.shape
    batch = own * COLS
    core, zh = lax.axis_index("core").astype(jnp.int32), lax.axis_index("zh").astype(jnp.int32)
    place = ((core * X + lax.axis_index("x")) * ZL + lax.axis_index("zl")).astype(jnp.int32)
    samples, core, zh, place, first = lax.optimization_barrier((samples, core, zh, place, core == 0))

    near = lax.all_gather(samples, "zh", axis=0, tiled=True)
    gathered = gather(near, "y", Y).reshape(X, ZL, CORE, share, win).transpose(2, 0, 1, 3, 4)
    mine = jnp.where(first, gathered[0], gathered[1]).reshape(batch // CORE, win)
    theirs = jnp.where(first, gathered[1], gathered[0]).reshape(batch // CORE, win)
    gathered = gathered.reshape(batch, win)

    def partial(rows):
        gram = lax.dot_general(rows, gathered, NT, preferred_element_type=f32)
        return jnp.concatenate([jnp.dot(rows, weight, preferred_element_type=f32), gram * GRAM_SCALE], axis=1)

    sums = lax.ppermute(partial(theirs).astype(f16), "core", SWAP).astype(f32) + partial(mine)
    for axis, size in (("x", X), ("zl", ZL)):
        blocks = sums.astype(f16).reshape(size, sums.shape[0] // size, sums.shape[1])
        sums = jnp.sum(exchange(blocks, axis).astype(f32), axis=0)

    packed = pack(place[None], sums, cotangent, row_second.reshape(-1, 128))
    for axis, size in (("zl", ZL), ("x", X)):
        packed = gather(packed, axis, size).reshape(packed.shape[0] * size, packed.shape[1])
    other = lax.ppermute(packed, "core", SWAP)
    early = make_early(packed, weight)

    message, seconds, slope, gram = make_message(core[None], early, packed, other, gathered, weight)
    message = exchange(message.astype(f16), "y").astype(f32)
    message, slope, gram, gathered = lax.optimization_barrier((message, slope, gram, gathered))
    keep, send = decoded(zh[None], message, win // 128)
    received = lax.ppermute(send.astype(f16), "zh", SWAP).astype(f32)

    grad, new_col, col_root = make_grad(gathered, slope, gram, col_second.reshape(-1, 128))
    input_grad, new_row, new_weight = update(
        own, keep, received, grad, weight, row_second, seconds, col_root
    )
    return (input_grad, new_weight, new_row.reshape(win), new_col.reshape(wout))


def solution(mesh):
    fine = Mesh(mesh.devices.reshape(X, ZL, CORE, Y, ZH), ("x", "zl", "core", "y", "zh"))
    row, col = ("x", "zl", "core"), ("y", "zh")
    in_specs = (P(col, row), P(row, col), P(row, col), P(row), P(col))
    out_specs = (P(col, row), P(row, col), P(row), P(col))
    return jax.shard_map(local, mesh=fine, in_specs=in_specs, out_specs=out_specs, check_vma=False)
```

```python
import functools

import jax
import jax.numpy as jnp
from jax import lax
from jax.experimental import pallas as pl
from jax.experimental.pallas import tpu as pltpu
from jax.sharding import Mesh
from jax.sharding import PartitionSpec as P

WIN = 36864
WOUT = 24576
ADAM_STEP = 10
WEIGHT_MAX = 0.03125
GRAM_SCALE = 1.0 / 32.0

X, ZL, CORE, Y, ZH = 4, 6, 2, 8, 2
ROWS = X * ZL * CORE
COLS = Y * ZH
f32, f16, bf16 = jnp.float32, jnp.float16, jnp.bfloat16


def silu_slope(preact):
    sig = jax.nn.sigmoid(preact)
    return sig * (1.0 + preact * (1.0 - sig))


def exchange(blocks, axis):
    return lax.all_to_all(blocks, axis, 0, 0)


def gather(block, axis, size):
    return exchange(jnp.broadcast_to(block[None], (size,) + block.shape), axis)


def exponent(bound):
    return jnp.ceil(jnp.log2(jnp.maximum(bound, 1e-30))) - 15.0


def split(value):
    high = lax.reduce_precision(value, 8, 7)
    return high.astype(bf16), value - high


def whole(value):
    return jnp.sum(jnp.sum(value, axis=0, keepdims=True), axis=1, keepdims=True)


SIDE = 16


def encode(grad_exp, rows, total):
    row_exp = exponent(jnp.max(jnp.max(rows, axis=0, keepdims=True), axis=1, keepdims=True))
    total_exp = exponent(total)
    rows = rows * jnp.exp2(-row_exp)
    rows_high = rows.astype(bf16).astype(f32)
    total = total * jnp.exp2(-total_exp)
    total_high = total.astype(bf16).astype(f32)
    lanes = lax.broadcasted_iota(jnp.int32, (1, 128), 1)
    scalars = jnp.zeros((1, 128), f32)
    for i, value in enumerate((grad_exp, row_exp, total_exp, total_high, (total - total_high) * 256.0)):
        scalars = jnp.where(lanes == i, value, scalars)
    pad = jnp.zeros((SIDE - 2 * rows.shape[0] - 1, 128), f32)
    return jnp.concatenate([rows_high, (rows - rows_high) * 256.0, scalars, pad], axis=0)


NT = (((1,), (1,)), ((), ()))


def halves(batch):
    return batch // 2 + batch // ROWS


def gram_kernel(rows_ref, others_ref, half_ref):
    width = half_ref.shape[1]
    share = rows_ref.shape[0] * CORE // ROWS
    rows = rows_ref[...]
    gram = [lax.dot_general(rows, side, NT, preferred_element_type=f32) for side in (rows, others_ref[...])]
    gram = jnp.concatenate(gram, axis=1) * GRAM_SCALE
    batch = gram.shape[1]
    for place in range(ROWS // CORE):
        part = slice(place * share, (place + 1) * share)
        half_ref[part, :] = pltpu.roll(gram[part, :], (batch - place * share) % batch, 1)[:, :width]


def make_gram(rows, others):
    batch = rows.shape[0] * CORE
    width = min(batch, -(-halves(batch) // 128) * 128)
    return pl.pallas_call(
        gram_kernel,
        out_shape=jax.ShapeDtypeStruct((rows.shape[0], width), f32),
        in_specs=[INSIDE] * 2,
        out_specs=INSIDE,
        compiler_params=pltpu.CompilerParams(vmem_limit_bytes=14 << 20),
    )(rows, others)


def pack_kernel(sums_ref, cotangent_ref, row_second_ref, packed_ref):
    share, wout = cotangent_ref.shape
    side = packed_ref.shape[1] - wout
    count = halves(share * ROWS)
    packed_ref[:, :wout] = (cotangent_ref[...].astype(f32) * silu_slope(sums_ref[:, :wout])).astype(bf16)
    gram = sums_ref[:, wout:]
    gram = jnp.concatenate([gram, jnp.zeros((share, side - gram.shape[1]), f32)], axis=1)
    high = gram.astype(bf16).astype(f32)
    low = pltpu.roll(gram - high, count, 1)
    lanes = lax.broadcasted_iota(jnp.int32, (share, side), 1)
    out = jnp.where(lanes < count, high, jnp.where(lanes < 2 * count, low, 0.0))
    rest = whole(row_second_ref[...])
    for i in range(3):
        part = rest.astype(bf16).astype(f32)
        rest = rest - part
        out = jnp.where(lanes == 2 * count + i, part, out)
    packed_ref[:, wout:] = out.astype(bf16)


def pack(sums, cotangent, row_second):
    share, wout = cotangent.shape
    width = wout + -(-(2 * halves(share * ROWS) + 3) // 128) * 128
    return pl.pallas_call(
        pack_kernel,
        out_shape=jax.ShapeDtypeStruct((share, width), bf16),
        in_specs=[INSIDE] * 3,
        out_specs=INSIDE,
        compiler_params=pltpu.CompilerParams(vmem_limit_bytes=16 << 20),
    )(sums, cotangent, row_second)


def early_kernel(mine_ref, weight_ref, early_ref):
    slope = mine_ref[:, : weight_ref.shape[1]]
    early_ref[...] = lax.dot_general(slope, weight_ref[...], NT, preferred_element_type=f32)


def make_early(mine, weight):
    rows, (win, wout) = mine.shape[0], weight.shape
    return pl.pallas_call(
        early_kernel,
        out_shape=jax.ShapeDtypeStruct((rows, win), f32),
        in_specs=[INSIDE] * 2,
        out_specs=INSIDE,
        compiler_params=pltpu.CompilerParams(vmem_limit_bytes=14 << 20),
        cost_estimate=pl.CostEstimate(flops=2 * rows * win * wout, bytes_accessed=2 * win * wout, transcendentals=0),
    )(mine, weight)


def message_kernel(core_ref, early_ref, mine_ref, other_ref, samples_ref, weight_ref,
                   message_ref, seconds_ref, slope_ref, gram_ref, partial_ref):
    batch, win = samples_ref.shape
    wout = weight_ref.shape[1]
    own = batch // COLS
    share = batch // ROWS
    half = batch // CORE
    first = core_ref[0] == 0
    packed_half = []
    for i, (low, high) in enumerate(((mine_ref, other_ref), (other_ref, mine_ref))):
        both = jnp.where(first, low[...], high[...])
        slope_ref[i * half : (i + 1) * half, :] = both[:, :wout]
        packed_half.append(both[:, wout:].astype(f32))
    packed_half = jnp.concatenate(packed_half, axis=0)
    slope = slope_ref[...]
    partial_ref[pl.ds(pl.multiple_of(core_ref[0] * half, 8), half), :] = early_ref[...]
    partial_ref[pl.ds(pl.multiple_of((1 - core_ref[0]) * half, 8), half), :] = lax.dot_general(
        other_ref[:, :wout], weight_ref[...], NT, preferred_element_type=f32
    )
    count = halves(batch)
    lanes = lax.broadcasted_iota(jnp.int32, packed_half.shape, 1)
    there = (lanes >= 2 * count) & (lanes < 2 * count + 3)
    seconds_ref[...] = whole(jnp.where(there, packed_half, 0.0)) * (1.0 / share)
    lanes = lax.broadcasted_iota(jnp.int32, (share, batch), 1)
    times = jnp.where(lanes < share, 1.0, jnp.where(lanes < batch // 2, 2.0, jnp.where(lanes < count, 1.0, 0.0)))
    for place in range(ROWS):
        piece = packed_half[place * share : (place + 1) * share, :]
        piece = piece + pltpu.roll(piece, piece.shape[1] - count, 1)
        gram_ref[place * share : (place + 1) * share, :] = pltpu.roll(piece[:, :batch] * times, place * share, 1)
    gram = gram_ref[...]
    mixed = lax.dot_general(slope, slope, NT, preferred_element_type=f32)
    total = whole(mixed * gram) * (1.0 / GRAM_SCALE)
    mixed_high = mixed.astype(bf16)
    mixed_low = (mixed - mixed_high.astype(f32)).astype(bf16)
    samples = samples_ref[...]
    spread = jnp.dot(mixed_high, samples, preferred_element_type=f32)
    spread += jnp.dot(mixed_low, samples, preferred_element_type=f32)
    row_total = jnp.sum(samples.astype(f32) * spread, axis=0, keepdims=True)

    top = jnp.max(jnp.max(jnp.abs(slope), axis=0, keepdims=True).astype(f32), axis=1, keepdims=True)
    grad_exp = exponent(top * (WEIGHT_MAX * wout))
    rows = jnp.concatenate([row_total[:, 128 * i : 128 * (i + 1)] for i in range(win // 128)], axis=0)
    side = encode(grad_exp, rows, total)
    factor = jnp.exp2(-grad_exp)
    each = own // share
    for dest in range(COLS):
        blocks = []
        for block in range(dest * each, (dest + 1) * each):
            start = ((block % CORE) * (ROWS // CORE) + block // CORE) * share
            blocks.append(partial_ref[start : start + share, :])
        grads = jnp.concatenate(blocks, axis=0) * factor
        for i in range(win // 128):
            start = (dest % ZH * (win // 128) + i) * own
            message_ref[dest // ZH, start : start + own, :] = grads[:, 128 * i : 128 * (i + 1)]
    for y in range(Y):
        message_ref[y, message_ref.shape[1] - SIDE :, :] = side


INSIDE, OUTSIDE = pl.BlockSpec(memory_space=pltpu.VMEM), pl.BlockSpec(memory_space=pltpu.HBM)
SCALAR = pl.BlockSpec(memory_space=pltpu.SMEM)


def make_message(core, early, mine, other, samples, weight):
    batch, win = samples.shape
    return pl.pallas_call(
        message_kernel,
        out_shape=(
            jax.ShapeDtypeStruct((Y, ZH * (batch // COLS) * (win // 128) + SIDE, 128), f32),
            jax.ShapeDtypeStruct((1, 1), f32),
            jax.ShapeDtypeStruct((batch, weight.shape[1]), bf16),
            jax.ShapeDtypeStruct((batch, batch), f32),
        ),
        in_specs=[SCALAR] + [INSIDE] * 5,
        out_specs=(INSIDE,) * 4,
        scratch_shapes=[pltpu.VMEM((batch, win), f32)],
        compiler_params=pltpu.CompilerParams(vmem_limit_bytes=20 << 20),
    )(core, early, mine, other, samples, weight)


def decode(sides, groups):
    scalars = jnp.concatenate([side[2 * groups : 2 * groups + 1, :] for side in sides], axis=0)
    powers = jnp.exp2(scalars)
    sums = jnp.zeros((groups, 128), f32)
    for i, side in enumerate(sides):
        sums += (side[:groups] + side[groups : 2 * groups] * (1.0 / 256.0)) * powers[i : i + 1, 1:2]
    total = whole((scalars[:, 3:4] + scalars[:, 4:5] * (1.0 / 256.0)) * powers[:, 2:3])
    factors = [powers[i : i + 1, 0:1] for i in range(len(sides))]
    return factors, sums, total, jnp.max(scalars[:, 0:1], axis=0, keepdims=True)


def decode_kernel(groups, zh_ref, message_ref, keep_ref, send_ref):
    zh = zh_ref[0]
    size = keep_ref.shape[0] - SIDE
    factors, sums, total, grad_exp = decode([message_ref[i, ZH * size :, :] for i in range(Y)], groups)

    def grads(half):
        rows = pl.ds(pl.multiple_of(half * size, 8), size)
        return sum(message_ref[i, rows, :] * factors[i] for i in range(Y))

    lanes = lax.broadcasted_iota(jnp.int32, (1, 128), 1)
    rows = [sums, jnp.where(lanes == 0, total, 0.0), jnp.zeros((SIDE - groups - 1, 128), f32)]
    keep_ref[:size, :] = grads(zh)
    keep_ref[size:, :] = jnp.concatenate(rows, axis=0)
    grad_exp += 3.0
    send_ref[:size, :] = grads(1 - zh) * jnp.exp2(-grad_exp)
    send_ref[size:, :] = encode(grad_exp, sums, total)


def decoded(zh, message, groups):
    size = (message.shape[1] - SIDE) // ZH + SIDE
    return pl.pallas_call(
        functools.partial(decode_kernel, groups),
        out_shape=(jax.ShapeDtypeStruct((size, 128), f32),) * 2,
        in_specs=[SCALAR, INSIDE],
        out_specs=(INSIDE,) * 2,
        compiler_params=pltpu.CompilerParams(vmem_limit_bytes=12 << 20),
    )(zh, message)


CHUNKS = 3


def grad_kernel(samples_ref, slope_ref, gram_ref, col_second_ref, grad_ref, new_col_ref, col_root_ref):
    win, wout = grad_ref.shape
    rows = win // CHUNKS
    gram = gram_ref[...]
    gram_high = gram.astype(bf16)
    gram_low = (gram - gram_high.astype(f32)).astype(bf16)
    columns = wout // CHUNKS
    for i in range(CHUNKS):
        part = slice(i * columns, (i + 1) * columns)
        slope = slope_ref[:, part]
        mixed = jnp.dot(gram_high, slope, preferred_element_type=f32)
        mixed += jnp.dot(gram_low, slope, preferred_element_type=f32)
        col_total = jnp.sum(slope.astype(f32) * mixed, axis=0, keepdims=True) * (1.0 / GRAM_SCALE)
        lines = slice(i * columns // 128, (i + 1) * columns // 128)
        second = jnp.concatenate([col_second_ref[j : j + 1, :] for j in range(lines.start, lines.stop)], axis=1)
        new_col = 0.999 * second + 0.001 * (col_total / WIN)
        new_col_ref[lines, :] = jnp.concatenate([new_col[:, j : j + 128] for j in range(0, columns, 128)], axis=0)
        col_root_ref[:, part] = jnp.sqrt(new_col)
    for i in range(CHUNKS):
        part = slice(i * rows, (i + 1) * rows)
        grad_ref[part, :] = lax.dot_general(
            samples_ref[:, part], slope_ref[...], (((0,), (0,)), ((), ())), preferred_element_type=f32
        )


def make_grad(samples, slope, gram, col_second):
    shape = (samples.shape[1], slope.shape[1])
    return pl.pallas_call(
        grad_kernel,
        out_shape=(
            jax.ShapeDtypeStruct(shape, f32),
            jax.ShapeDtypeStruct(col_second.shape, f32),
            jax.ShapeDtypeStruct((1, shape[1]), f32),
        ),
        in_specs=[INSIDE] * 4,
        out_specs=(INSIDE,) * 3,
        compiler_params=pltpu.CompilerParams(vmem_limit_bytes=14 << 20),
    )(samples, slope, gram, col_second)


def update_kernel(keep_ref, received_ref, grad_ref, old_ref, row_second_ref, seconds_ref, col_root_ref,
                  input_grad_ref, new_row_ref, new_weight_ref, root_ref, new_ref, sems):
    win, wout = old_ref.shape
    groups = win // 128
    rows = win // CHUNKS

    def store(i):
        part = pl.ds(i * rows, rows)
        return pltpu.make_async_copy(new_ref.at[part], new_weight_ref.at[part], sems.at[i])

    own = input_grad_ref.shape[0]
    size = own * groups
    factors, sums, total, _ = decode([received_ref[size:, :]], groups)
    for i in range(groups):
        part = slice(i * own, (i + 1) * own)
        grads = received_ref[part, :] * factors[0] + keep_ref[part, :]
        input_grad_ref[:, 128 * i : 128 * (i + 1)] = grads.astype(bf16)
    sums += keep_ref[size : size + groups, :]
    total += keep_ref[size + groups : size + groups + 1, :1]
    new_row = 0.999 * row_second_ref[...] + 0.001 * (sums / WOUT)
    new_row_ref[...] = new_row
    scale = 0.999 * (seconds_ref[...] / WIN) + 0.001 * (total / WOUT / WIN)
    root = 100.0 * jnp.sqrt(new_row / (scale * (1.0 - 0.999**ADAM_STEP)))
    for i in range(groups):
        root_ref[128 * i : 128 * (i + 1), :] = jnp.transpose(jnp.broadcast_to(root[i : i + 1], (128, 128)))

    for i in range(CHUNKS):
        part = slice(i * rows, (i + 1) * rows)
        root = root_ref[part, :]
        for j in range(0, wout, 128):
            bottom = root * col_root_ref[:, j : j + 128] + 1e-06
            change = grad_ref[part, j : j + 128] / bottom
            new_ref[part, j : j + 128] = (old_ref[part, j : j + 128].astype(f32) - change).astype(bf16)
        store(i).start()
    for i in range(CHUNKS):
        store(i).wait()


def update(own, keep, received, grad, weight, row_second, seconds, col_root):
    win, wout = weight.shape
    return pl.pallas_call(
        update_kernel,
        out_shape=(
            jax.ShapeDtypeStruct((own, win), bf16),
            jax.ShapeDtypeStruct((win // 128, 128), f32),
            jax.ShapeDtypeStruct((win, wout), bf16),
        ),
        in_specs=[INSIDE] * 7,
        out_specs=(INSIDE, INSIDE, OUTSIDE),
        scratch_shapes=[
            pltpu.VMEM((win, 128), f32),
            pltpu.VMEM((win, wout), bf16),
            pltpu.SemaphoreType.DMA((CHUNKS,)),
        ],
        compiler_params=pltpu.CompilerParams(vmem_limit_bytes=14 << 20),
    )(keep, received, grad, weight, row_second.reshape(-1, 128), seconds, col_root)


SWAP = ((0, 1), (1, 0))


def local(samples, cotangent, weight, row_second, col_second):
    own, win = samples.shape
    share, wout = cotangent.shape
    batch = own * COLS
    core, zh = lax.axis_index("core").astype(jnp.int32), lax.axis_index("zh").astype(jnp.int32)
    samples, core, zh, first = lax.optimization_barrier((samples, core, zh, core == 0))

    near = lax.all_gather(samples, "zh", axis=0, tiled=True)
    gathered = gather(near, "y", Y).reshape(X, ZL, CORE, share, win).transpose(2, 0, 1, 3, 4)
    mine = jnp.where(first, gathered[0], gathered[1]).reshape(batch // CORE, win)
    theirs = jnp.where(first, gathered[1], gathered[0]).reshape(batch // CORE, win)
    gathered = gathered.reshape(batch, win)

    def partial(rows, others):
        product = jnp.dot(rows, weight, preferred_element_type=f32)
        return jnp.concatenate([product, make_gram(rows, others)], axis=1)

    sums = lax.ppermute(partial(theirs, mine).astype(f16), "core", SWAP).astype(f32) + partial(mine, theirs)
    for axis, size in (("x", X), ("zl", ZL)):
        blocks = sums.astype(f16).reshape(size, sums.shape[0] // size, sums.shape[1])
        sums = jnp.sum(exchange(blocks, axis).astype(f32), axis=0)

    packed = pack(sums, cotangent, row_second.reshape(-1, 128))
    for axis, size in (("zl", ZL), ("x", X)):
        packed = gather(packed, axis, size).reshape(packed.shape[0] * size, packed.shape[1])
    other = lax.ppermute(packed, "core", SWAP)
    early = make_early(packed, weight)

    message, seconds, slope, gram = make_message(core[None], early, packed, other, gathered, weight)
    message = exchange(message.astype(f16), "y").astype(f32)
    message, slope, gram, gathered = lax.optimization_barrier((message, slope, gram, gathered))
    keep, send = decoded(zh[None], message, win // 128)
    received = lax.ppermute(send.astype(f16), "zh", SWAP).astype(f32)

    grad, new_col, col_root = make_grad(gathered, slope, gram, col_second.reshape(-1, 128))
    input_grad, new_row, new_weight = update(
        own, keep, received, grad, weight, row_second, seconds, col_root
    )
    return (input_grad, new_weight, new_row.reshape(win), new_col.reshape(wout))


def solution(mesh):
    fine = Mesh(mesh.devices.reshape(X, ZL, CORE, Y, ZH), ("x", "zl", "core", "y", "zh"))
    row, col = ("x", "zl", "core"), ("y", "zh")
    in_specs = (P(col, row), P(row, col), P(row, col), P(row), P(col))
    out_specs = (P(col, row), P(row, col), P(row), P(col))
    return jax.shard_map(local, mesh=fine, in_specs=in_specs, out_specs=out_specs, check_vma=False)
```
